128 devices in a mesh: section: 8 (over y, x_lo), tp: 16 (over z, x_hi, core).
Axes of the slice: x: 4 (x_hi: 2, x_lo: 2; x = x_hi * 2 + x_lo), y: 4, z: 4, core: 2. Of those that a mesh axis runs over, the one named last changes fastest.
Arguments:
- hidden: bfloat16 [8, 256, 8192], P('section', 'tp'), may hold values from -4 to 4
- tiles: bfloat16 [256, 8192], P(('section', 'tp')), may hold values from -8 to 8
- tile_counts: int32 [4], replicated, may hold values from 1 to 4, 8 in all
- sample_order: int32 [4], replicated, may hold values from 0 to 3, each once
- query_weight: bfloat16 [8, 8192, 8192], P('section', None, 'tp'), may hold values from -0.0625 to 0.0625
- tile_weight: bfloat16 [8, 8192, 2048], P('section', None, 'tp'), may hold values from -0.0625 to 0.0625
- output_weight: bfloat16 [8, 8192, 8192], P('section', 'tp'), may hold values from -0.0625 to 0.0625
- head_gains: float32 [8, 2, 128], P('section'), may hold values from 0.5 to 2
- cross_gate: float32 [8], P('section'), may hold values from 0.5 to 2
- cotangent: bfloat16 [8, 256, 8192], P('section', 'tp'), may hold values from -3 to 3
Outputs:
- out_hidden: bfloat16 [8, 256, 8192], P('section', 'tp')
- hidden_grad: bfloat16 [8, 256, 8192], P('section', 'tp')
- tile_grad: float32 [256, 8192], P(('section', 'tp'))
The draws below stay inside these ranges and needn't reach their ends.
Inputs may be any that keep to these rules, and one draw needn't show every extreme that they name: tile_counts add up to 8; sample s's tiles follow those of samples 0 to s - 1 in the packed tile rows. `sample_order`: every sample appears once.
All inputs are finite; a program needn't handle non-finite values.
Results may differ from the reference program's by a relative error of at most 0.018.
Values may be sent and summed in bfloat16 or wider, within the bound.
A program may use at most 128 MiB of HBM per device.

```python
import math
import jax
import jax.numpy as jnp
import numpy as np
from jax import lax

D = 8192
HEADS = 64
KV_HEADS = 8
HD = 128
MAX_TILES = 4
LEN = 64
PATCH = 32
SAMPLES = 4
TOK = 256
NTILES = 8
TILE_ROWS = 256
GROUP_HEADS = 4
N_SECTION = 8
N_TP = 16


def draw_hidden(key, part):
    key = jax.random.fold_in(key, 11)
    key_values, key_rows = jax.random.split(key, 2)
    shape = (N_SECTION, TOK, D)
    row_scale = jnp.exp(jax.random.uniform(key_rows, (N_SECTION, TOK, 1), jnp.float32, math.log(0.1), 0.0))
    values = jnp.clip(jax.random.normal(key_values, shape, jnp.float32), -3.5, 3.5)
    return (values * row_scale).astype(jnp.bfloat16)


def draw_tiles(key, part):
    key = jax.random.fold_in(key, 12)
    key_values, key_rows = jax.random.split(key, 2)
    shape = (TILE_ROWS, D)
    row_scale = jnp.exp(jax.random.uniform(key_rows, (TILE_ROWS, 1), jnp.float32, math.log(0.2), math.log(2.0)))
    values = jnp.clip(jax.random.normal(key_values, shape, jnp.float32), -3.5, 3.5)
    return (values * row_scale).astype(jnp.bfloat16)


def level_of(rng, shape, shards, low, largest):
    loudness = 1.0
    for dim, parts in shards:
        heights = jax.random.uniform(jax.random.fold_in(jax.random.fold_in(rng, 6), dim), (parts,), jnp.float32, low / len(shards), largest / len(shards))
        loudness = loudness * jnp.repeat(jnp.exp(heights), shape[dim] // parts).reshape((-1,) + (1,) * (len(shape) - 1 - dim))
    return loudness


def profile(amount, total, limit, slope):
    weights = [(1 << 20) // math.isqrt(grade ** slope) + 1 for grade in range(2, amount + 1)]
    surplus, given = total - limit - (amount - 1), [1] * (amount - 1)
    while surplus > 0:
        candidates = [i for i in range(amount - 1) if given[i] < limit]
        pool, budget = sum([weights[i] for i in candidates]), surplus
        for i in candidates:
            extra = min(limit - given[i], max(1, budget * weights[i] // pool), surplus)
            given[i] = given[i] + extra
            surplus = surplus - extra
    return np.array([limit] + given)


def uneven(own_key, count, total, reach, lean):
    if count == 2:
        one = jax.random.randint(own_key, (), max(1, total - reach), min(reach, total - 1) + 1)
        return jnp.stack([one, total - one])
    lengths = jnp.asarray(profile(count, total, reach, lean), jnp.int32)
    couples = (count - 1) // 2
    source_of, sink = lengths[1:1 + 2 * couples:2], lengths[2:2 + 2 * couples:2]
    slack = jnp.minimum(source_of - 1, reach - sink)
    shifted = jax.random.randint(jax.random.fold_in(own_key, 1), (couples,), 0, 1 << 20) % (slack + 1)
    lengths = lengths.at[1:1 + 2 * couples:2].set(source_of - shifted).at[2:2 + 2 * couples:2].set(sink + shifted)
    return lengths[jax.random.permutation(jax.random.fold_in(own_key, 2), count)]


def scatter_about(stream_key, extent, spread, reach, shards=(), kind=jnp.bfloat16):
    entries = jax.random.normal(stream_key, extent, jnp.float32) * spread
    if len(shards) > 0:
        entries = level_of(stream_key, extent, shards, -0.22, 0.18) * entries
    return jnp.clip(entries, min=-reach, max=reach).astype(kind)


def setup_inputs(seed: int = 0) -> dict:
    key_of = jax.random.split(jax.random.key(seed), 11)
    return {
        "hidden": draw_hidden(jax.random.fold_in(key_of[10], 71), 0),
        "tiles": draw_tiles(jax.random.fold_in(key_of[10], 71), 0),
        "tile_counts": uneven(key_of[2], SAMPLES, NTILES, MAX_TILES, 2).astype(jnp.int32),
        "sample_order": jax.random.permutation(key_of[3], SAMPLES).astype(jnp.int32),
        "query_weight": scatter_about(key_of[4], (N_SECTION, D, D), D ** -0.5, 0.0625, ((0, 8), (2, 16))),
        "tile_weight": scatter_about(key_of[5], (N_SECTION, D, 2 * KV_HEADS * HD), D ** -0.5, 0.0625, ((0, 8), (2, 16))),
        "output_weight": scatter_about(key_of[6], (N_SECTION, D, D), D ** -0.5, 0.0625, ((0, 8), (1, 16))),
        "head_gains": jnp.clip(jnp.exp(math.log(2.0) - 1.3862944 * jax.random.uniform(key_of[7], (N_SECTION, 2, HD), jnp.float32) ** level_of(key_of[7], (N_SECTION, 2, HD), ((0, 8),), -0.2, 0.2)), 0.5, 2.0),
        "cross_gate": jnp.clip(0.5 + 1.5 * jax.random.uniform(key_of[8], (N_SECTION,), jnp.float32) ** level_of(key_of[8], (N_SECTION,), ((0, 8),), -0.2, 0.2), 0.5, 2.0),
        "cotangent": scatter_about(key_of[9], (N_SECTION, TOK, D), 0.5, 3.0, ((0, 8), (1, 16))),
    }


NORM_EPS = 1e-06

def head_norm(values, gain):
    scale = lax.rsqrt(lax.optimization_barrier(jnp.mean(values * values, axis=-1, keepdims=True)) + NORM_EPS)
    return (values * scale * gain, scale)

def head_norm_back(values, scale, gain, grad):
    normed = values * scale
    scaled = grad * gain
    return scale * (scaled - normed * lax.optimization_barrier(jnp.mean(normed * scaled, axis=-1, keepdims=True)))

def widen(values):
    return lax.optimization_barrier(values).astype(jnp.float32)

def linked_rows(tile_counts, sample_order):
    ends = jnp.cumsum(tile_counts).astype(jnp.int32)
    tile_index = jnp.arange(TILE_ROWS, dtype=jnp.int32) // PATCH
    tile_sample = lax.optimization_barrier(jnp.sum((tile_index[:, None] >= ends[None, :]).astype(jnp.int32), axis=1))
    position = jnp.arange(TOK, dtype=jnp.int32) // LEN
    picks = position[:, None] == jnp.arange(SAMPLES, dtype=jnp.int32)[None, :]
    token_sample = lax.optimization_barrier(jnp.sum(jnp.where(picks, sample_order[None, :], 0), axis=1))
    return token_sample[:, None] == tile_sample[None, :]

def section_pass(text_rows, tiles, linked, query_matrix, tile_matrix, output_matrix, gains, gate_logit, grad_rows):
    split = N_TP // KV_HEADS
    query_gain = gains[0] * HD ** (-0.5)
    key_gain = gains[1]
    gate = jnp.tanh(gate_logit)
    queries = jnp.dot(text_rows, query_matrix, preferred_element_type=jnp.float32).reshape(TOK, HEADS, HD)
    query_normed, query_scale = head_norm(queries, query_gain)
    normed_queries = widen(query_normed.astype(jnp.bfloat16)).reshape(TOK, KV_HEADS, split, GROUP_HEADS, HD)
    projected = jnp.dot(tiles, tile_matrix, preferred_element_type=jnp.float32).reshape(TILE_ROWS, KV_HEADS, 2, HD)
    key_raw = jnp.transpose(projected[:, :, 0, :], (1, 0, 2))
    key_normed, key_scale = head_norm(key_raw, key_gain)
    keys = widen(key_normed.astype(jnp.bfloat16))
    values = widen(jnp.transpose(projected[:, :, 1, :], (1, 0, 2)).astype(jnp.bfloat16))
    scores = jnp.einsum('tkpgd,krd->kpgtr', normed_queries, keys)
    raised = jnp.where(linked, jnp.exp(scores), 0.0)
    weights = widen((raised / lax.optimization_barrier(jnp.sum(raised, axis=-1, keepdims=True))).astype(jnp.bfloat16))
    attended = jnp.einsum('kpgtr,krd->tkpgd', weights, values).astype(jnp.bfloat16).reshape(TOK, HEADS * HD)
    branch = jnp.dot(attended, output_matrix, preferred_element_type=jnp.float32)
    out_rows = (text_rows.astype(jnp.float32) + gate * branch).astype(jnp.bfloat16)
    grad_text = jnp.dot(grad_rows, output_matrix.T, preferred_element_type=jnp.float32)
    grad_out = widen((gate * grad_text).astype(jnp.bfloat16)).reshape(TOK, KV_HEADS, split, GROUP_HEADS, HD)
    grad_prob = jnp.einsum('tkpgd,krd->kpgtr', grad_out, values)
    center = lax.optimization_barrier(jnp.sum(weights * grad_prob, axis=-1, keepdims=True))
    grad_score = widen((weights * (grad_prob - center)).astype(jnp.bfloat16))
    grad_normed = jnp.einsum('kpgtr,krd->tkpgd', grad_score, keys).reshape(TOK, HEADS, HD)
    grad_query = head_norm_back(queries, query_scale, query_gain, grad_normed).astype(jnp.bfloat16).reshape(TOK, HEADS * HD)
    grad_input = jnp.dot(grad_query, query_matrix.T, preferred_element_type=jnp.float32)
    hidden_grad = (grad_rows.astype(jnp.float32) + grad_input).astype(jnp.bfloat16)
    grad_keys = widen(jnp.einsum('kpgtr,tkpgd->kprd', grad_score, normed_queries).astype(jnp.bfloat16))
    grad_values = jnp.einsum('kpgtr,tkpgd->kprd', weights, grad_out).astype(jnp.bfloat16)
    grad_key_raw = head_norm_back(key_raw[:, None], key_scale[:, None], key_gain, grad_keys).astype(jnp.bfloat16)
    stacked = widen(jnp.stack([grad_key_raw, grad_values], axis=2))
    matrix_full = tile_matrix.astype(jnp.float32).reshape(D, KV_HEADS, 2, HD)
    term = jnp.einsum('kpcrd,ekcd->re', stacked, matrix_full)
    return (out_rows, hidden_grad, term)

def reference(hidden, tiles, tile_counts, sample_order, query_weight, tile_weight, output_weight, head_gains, cross_gate, cotangent):
    linked = linked_rows(tile_counts, sample_order)

    def one_section(total, inputs):
        text_rows, query_matrix, tile_matrix, output_matrix, gains, gate_logit, grad_rows = inputs
        out_rows, hidden_grad, term = section_pass(text_rows, tiles, linked, query_matrix, tile_matrix, output_matrix, gains, gate_logit, grad_rows)
        return (total + term, (out_rows, hidden_grad))
    initial = jnp.zeros((TILE_ROWS, D), jnp.float32)
    tile_grad, (out_hidden, hidden_grad) = lax.scan(one_section, initial, (hidden, query_weight, tile_weight, output_weight, head_gains, cross_gate, cotangent))
    return (out_hidden, hidden_grad, tile_grad)
```

```python
import functools
import jax
import jax.numpy as jnp
from jax import lax
from jax.experimental import pallas as pl
from jax.experimental.pallas import tpu as pltpu
from jax.sharding import PartitionSpec as P

MESH = pl.DeviceIdType.MESH
NORM_EPS = 1e-06
D = 8192
HD = 128
LOCAL = 512
HEADS = 4
ROWS = 256
BF = jnp.bfloat16
F32 = jnp.float32

XZ = ((0, 2304, 768), (2304, 2304, 768))
ZX = ((4608, 1792, 896), (6400, 1792, 896))
PIECE = 512


def contract_last(left, right):
    return lax.dot_general(left, right, (((1,), (1,)), ((), ())), preferred_element_type=F32)


def contract_first(left, right):
    return lax.dot_general(left, right, (((0,), (0,)), ((), ())), preferred_element_type=F32)


def norm_scale(values):
    return lax.rsqrt(jnp.mean(values * values, axis=-1, keepdims=True) + NORM_EPS)


def head_norm_back(values, scale, gain, grad):
    normed = values * scale
    scaled = grad * gain
    return scale * (scaled - normed * jnp.mean(normed * scaled, axis=-1, keepdims=True))


def add_to(total, *terms):
    value = total[...].astype(F32)
    for term in terms:
        value = value + term[...].astype(F32)
    total[...] = value.astype(total.dtype)


def kernel(
    counts, order, gate_ref, gains, hid, cot, til, wq_hbm, wt_hbm, wo_hbm,
    out_ref, grad_ref, tgrad_ref,
    wq, wt, wo, hfull, cfull, tfull,
    sib_o, rel_o, zin_o, xin_o,
    sib_g, rel_g, zin_g, xin_g,
    sib_t, yrel, yin, xin_t, zin_t,
    tin, flat, block, gin,
    queries, gradout, normedq, weights, attended, gradq, proj, kv, gxin, gxout, mask,
    load_sem, send_sem, recv_sem,
):
    sec = lax.axis_index("section")
    tp = lax.axis_index("tp")
    y, xl = lax.div(sec, 2), lax.rem(sec, 2)
    z, xh, c = lax.div(tp, 4), lax.rem(lax.div(tp, 2), 2), lax.rem(tp, 2)
    x = xh * 2 + xl
    zh, zl = lax.div(z, 2), lax.rem(z, 2)
    member = lax.rem(tp, 8)
    oc, ox = 1 - c, 1 - xh

    def turn(value, by):
        return lax.rem(value + by, 4)

    def device(dx=0, dy=0, dz=0, core=None):
        nx, ny, nz = turn(x, dx), turn(y, dy), turn(z, dz)
        core = c if core is None else core
        return (ny * 2 + lax.rem(nx, 2), nz * 4 + lax.div(nx, 2) * 2 + core)

    def mate(step):
        return lax.rem(member + step, 8)

    sib = device(core=oc)
    xpair = device(dx=2)
    zup, zdown, zfar = device(dz=1), device(dz=3), device(dz=2)
    yup, ydown = device(dy=1), device(dy=3)
    xup, xdown = device(dx=1), device(dx=3)

    loads = []
    for i, (src, dst) in enumerate(((wq_hbm, wq), (wt_hbm, wt), (wo_hbm, wo))):
        loads.append(pltpu.make_async_copy(src, dst, load_sem.at[i]))
        loads[-1].start()

    barrier = pltpu.get_barrier_semaphore()
    zodd = device(dz=lax.rem(zl * 2 + 3, 4))
    greeted = [(sec, zh * 8 + mate(step)) for step in range(1, 8)]
    greeted += [zodd, zfar, yup, ydown, xup, xdown]
    for other in greeted:
        pl.semaphore_signal(barrier, inc=1, device_id=other, device_id_type=MESH)

    hfull[c, z, xh] = hid[...]
    cfull[c, z, xh] = cot[...]

    tile_index = lax.div(lax.broadcasted_iota(jnp.int32, (1, ROWS), 1), 32)
    tile_sample = jnp.zeros((1, ROWS), jnp.int32)
    end = jnp.int32(0)
    for i in range(4):
        end = end + counts[i]
        tile_sample = tile_sample + (tile_index >= end).astype(jnp.int32)
    for i in range(4):
        row = (tile_sample == order[i]).astype(F32)
        for half in range(2):
            mask[pl.ds(half * 128 + i * 32, 32), :] = jnp.broadcast_to(row, (32, ROWS))
    gate = jnp.tanh(jnp.full((1, HD), gate_ref[0], F32))
    query_gain = gains[0:1, :] * HD ** (-0.5)
    key_gain = gains[1:2, :]

    pl.semaphore_wait(barrier, len(greeted))

    used = [0]

    def send(src, dst, target):
        i = used[0]
        used[0] += 1
        copy = pltpu.make_async_remote_copy(
            src_ref=src, dst_ref=dst, send_sem=send_sem.at[i], recv_sem=recv_sem.at[i],
            device_id=target, device_id_type=MESH,
        )
        copy.start()
        return copy

    def here(ref, target):
        return send(ref, ref, target)

    def sent(copies):
        for copy in copies:
            copy.wait_send()

    def gather_xz(full, part, use):
        col, width, _ = part
        cols = pl.ds(col, width)
        low, high = pl.ds(col, width // 2), pl.ds(col + width // 2, width // 2)
        a = here(full.at[c, z, xh, :, cols], xpair)
        yield
        a.wait_recv()
        up = here(full.at[c, z, :, :, cols], zup)
        down = here(full.at[c, z, :, :, cols], zdown)
        yield
        up.wait_recv()
        up2 = here(full.at[c, turn(z, 3), :, :, low], zup)
        down.wait_recv()
        down2 = here(full.at[c, turn(z, 1), :, :, high], zdown)
        yield
        up2.wait_recv()
        down2.wait_recv()
        s = here(full.at[c, :, :, :, cols], sib)
        yield
        s.wait_recv()
        use(part)
        sent([a, up, down, up2, down2, s])
        yield

    def gather_zx(full, part, use):
        col, width, _ = part
        cols = pl.ds(col, width)
        low, high = pl.ds(col, width // 2), pl.ds(col + width // 2, width // 2)
        mine = full.at[c, z, xh, :, cols]
        up, down, a = here(mine, zup), here(mine, zdown), here(mine, xpair)
        yield
        up.wait_recv()
        up2 = here(full.at[c, turn(z, 3), xh, :, low], zup)
        a1 = here(full.at[c, turn(z, 3), xh, :, cols], xpair)
        down.wait_recv()
        down2 = here(full.at[c, turn(z, 1), xh, :, high], zdown)
        a2 = here(full.at[c, turn(z, 1), xh, :, cols], xpair)
        yield
        up2.wait_recv()
        down2.wait_recv()
        a3 = here(full.at[c, turn(z, 2), xh, :, cols], xpair)
        yield
        for copy in (a, a1, a2, a3):
            copy.wait_recv()
        s = here(full.at[c, :, :, :, cols], sib)
        yield
        s.wait_recv()
        use(part)
        sent([up, down, a, up2, a1, down2, a2, a3, s])
        yield

    def use_hidden(part):
        col, width, step = part

        def one(i, carry):
            at = pl.ds(pl.multiple_of(col + i * step, 128), step)
            rows = hfull[:, :, :, :, at].reshape(ROWS, step)
            queries[...] += jnp.dot(rows, wq[at, :], preferred_element_type=F32)
            return carry

        lax.fori_loop(0, width // step, one, 0)

    def use_cot(part):
        col, width, step = part

        def one(i, carry):
            at = pl.ds(pl.multiple_of(col + i * step, 128), step)
            rows = cfull[:, :, :, :, at].reshape(ROWS, step)
            gradout[...] += contract_last(rows, wo[:, at])
            return carry

        lax.fori_loop(0, width // step, one, 0)

    def tblock(full, yy, xx):
        return full.at[c, yy, lax.div(xx, 2), lax.rem(xx, 2)]

    def gather_tiles():
        copies = []
        for step in range(1, 8):
            j = mate(step)
            copies.append(send(til.at[j], tin.at[step], (sec, zh * 8 + j)))
        yield
        for copy in copies:
            copy.wait_recv()
        tin[0] = til[member]
        for s in range(8):
            owner = lax.rem(member + 8 - s, 8)
            flat[pl.ds(pl.multiple_of(owner * 16, 16), 16), :] = tin[s].astype(F32)
        for r in range(2):
            for b in range(8):
                block[b, pl.ds(r, 8, stride=2), :] = flat[pl.ds(r * 8 + b, 8, stride=16), :]
        own = tfull.at[c, y, xh, xl, zh, zl]
        for b in range(8):
            own[:, pl.ds(b * 128, 128)] = block[b].astype(BF)
        zs = [here(own, zup), here(own, zdown), here(own, zfar)]
        yield
        for copy in zs:
            copy.wait_recv()
        mine = tblock(tfull, y, x)
        xs = [here(mine, xup), here(mine, xdown), here(mine, xpair)]
        ups, downs = [here(mine, yup)], [here(mine, ydown)]
        yield
        for copy, by in zip(xs, (3, 1, 2)):
            copy.wait_recv()
            got = tblock(tfull, y, turn(x, by))
            ups.append(here(got, yup))
            downs.append(here(got, ydown))
        sibs = [here(tfull.at[c, y], sib)]
        yield
        far = []
        for k, by in enumerate((0, 3, 1, 2)):
            ups[k].wait_recv()
            downs[k].wait_recv()
            if k % 2 == 0:
                far.append(here(tblock(tfull, turn(y, 3), turn(x, by)), yup))
            else:
                far.append(here(tblock(tfull, turn(y, 1), turn(x, by)), ydown))
        sibs.append(here(tfull.at[c, turn(y, 3)], sib))
        sibs.append(here(tfull.at[c, turn(y, 1)], sib))
        yield
        for copy in far:
            copy.wait_recv()
        sibs.append(here(tfull.at[c, turn(y, 2)], sib))
        yield
        for copy in sibs:
            copy.wait_recv()
        sent(copies + zs + xs + ups + downs + far + sibs)
        yield

    def scatter_xz(full, sibin, rel, zin, xin, part, make, finish):
        col, width, _ = part
        cols = pl.ds(col, width)
        low, high = pl.ds(col, width // 2), pl.ds(col + width // 2, width // 2)
        make(part)
        s = send(full.at[oc, :, :, :, cols], sibin.at[:, :, :, cols], sib)
        yield
        s.wait_recv()
        add_to(full.at[c, turn(z, 2), :, :, cols], sibin.at[turn(z, 2), :, :, cols])
        r0 = send(full.at[c, turn(z, 2), :, :, low], rel.at[0, :, :, low], zup)
        r1 = send(full.at[c, turn(z, 2), :, :, high], rel.at[1, :, :, high], zdown)
        for by in (1, 3, 0):
            add_to(full.at[c, turn(z, by), :, :, cols], sibin.at[turn(z, by), :, :, cols])
        yield
        r0.wait_recv()
        add_to(full.at[c, turn(z, 1), :, :, low], rel.at[0, :, :, low])
        z0 = send(full.at[c, turn(z, 1), :, :, cols], zin.at[0, :, :, cols], zup)
        r1.wait_recv()
        add_to(full.at[c, turn(z, 3), :, :, high], rel.at[1, :, :, high])
        z1 = send(full.at[c, turn(z, 3), :, :, cols], zin.at[1, :, :, cols], zdown)
        yield
        z0.wait_recv()
        z1.wait_recv()
        add_to(full.at[c, z, ox, :, cols], zin.at[0, ox, :, cols], zin.at[1, ox, :, cols])
        a = send(full.at[c, z, ox, :, cols], xin.at[0, :, cols], xpair)
        yield
        a.wait_recv()
        finish(cols, (full.at[c, z, xh, :, cols], zin.at[0, xh, :, cols], zin.at[1, xh, :, cols], xin.at[0, :, cols]))
        sent([s, r0, r1, z0, z1, a])
        yield

    def scatter_zx(full, sibin, rel, zin, xin, part, make, finish):
        col, width, _ = part
        cols = pl.ds(col, width)
        low, high = pl.ds(col, width // 2), pl.ds(col + width // 2, width // 2)
        make(part)
        s = send(full.at[oc, :, :, :, cols], sibin.at[:, :, :, cols], sib)
        yield
        s.wait_recv()
        add_to(full.at[c, :, ox, :, cols], sibin.at[:, ox, :, cols])
        a = send(full.at[c, :, ox, :, cols], xin.at[:, :, cols], xpair)
        yield
        a.wait_recv()
        add_to(full.at[c, turn(z, 2), xh, :, cols], sibin.at[turn(z, 2), xh, :, cols], xin.at[turn(z, 2), :, cols])
        r0 = send(full.at[c, turn(z, 2), xh, :, low], rel.at[0, 0, :, low], zup)
        r1 = send(full.at[c, turn(z, 2), xh, :, high], rel.at[1, 0, :, high], zdown)
        for by in (1, 3):
            add_to(full.at[c, turn(z, by), xh, :, cols], sibin.at[turn(z, by), xh, :, cols], xin.at[turn(z, by), :, cols])
        yield
        r0.wait_recv()
        add_to(full.at[c, turn(z, 1), xh, :, low], rel.at[0, 0, :, low])
        z0 = send(full.at[c, turn(z, 1), xh, :, cols], zin.at[0, 0, :, cols], zup)
        r1.wait_recv()
        add_to(full.at[c, turn(z, 3), xh, :, high], rel.at[1, 0, :, high])
        z1 = send(full.at[c, turn(z, 3), xh, :, cols], zin.at[1, 0, :, cols], zdown)
        yield
        z0.wait_recv()
        z1.wait_recv()
        finish(cols, (full.at[c, z, xh, :, cols], sibin.at[z, xh, :, cols], xin.at[z, :, cols], zin.at[0, 0, :, cols], zin.at[1, 0, :, cols]))
        sent([s, a, r0, r1, z0, z1])
        yield

    def total(terms):
        value = terms[0][...].astype(F32)
        for term in terms[1:]:
            value = value + term[...].astype(F32)
        return value

    def make_out(part):
        col, width, _ = part

        def one(i, carry):
            at = pl.ds(pl.multiple_of(col + i * 256, 128), 256)
            value = jnp.dot(attended[...], wo[:, at], preferred_element_type=F32)
            hfull[:, :, :, :, at] = value.astype(BF).reshape(2, 4, 2, 16, 256)
            return carry

        lax.fori_loop(0, width // 256, one, 0)

    def finish_out(cols, terms):
        out_ref[:, cols] = (hid[:, cols].astype(F32) + gate[0:1, 0:1] * total(terms)).astype(BF)

    def make_grad(part):
        col, width, _ = part

        def one(i, carry):
            at = pl.ds(pl.multiple_of(col + i * 256, 128), 256)
            value = contract_last(gradq[...], wq[at, :])
            cfull[:, :, :, :, at] = value.astype(BF).reshape(2, 4, 2, 16, 256)
            return carry

        lax.fori_loop(0, width // 256, one, 0)

    def finish_grad(cols, terms):
        grad_ref[:, cols] = (cot[:, cols].astype(F32) + total(terms)).astype(BF)

    def scatter_tiles(col):
        cols = pl.ds(col, PIECE)

        def unit(ref, *index):
            return ref.at[(*index, Ellipsis, cols)]

        for core in (oc, c):
            for h in range(2):
                for l in range(2):
                    at = (l * 4 + h * 2 + core) * 1024 + col
                    value = contract_last(gxout[...], wt[pl.ds(pl.multiple_of(at, 128), PIECE), :])
                    tfull[core, :, h, :, :, l, :, cols] = value.astype(BF).reshape(4, 2, 2, 16, PIECE)
            if core is oc:
                s = send(tfull.at[oc, :, :, :, :, :, :, cols], sib_t.at[:, :, :, :, :, :, cols], sib)
        yield
        s.wait_recv()

        def merge(by):
            yy = turn(y, by)
            for h in range(2):
                add_to(tfull.at[c, yy, h, :, :, :, :, cols], sib_t.at[yy, h, :, :, :, :, cols])

        merge(2)
        r0 = send(tfull.at[c, turn(y, 2), 0, :, :, :, :, cols], yrel.at[0, :, :, :, :, cols], yup)
        r1 = send(tfull.at[c, turn(y, 2), 1, :, :, :, :, cols], yrel.at[1, :, :, :, :, cols], ydown)
        for by in (1, 3, 0):
            merge(by)
        yield
        r0.wait_recv()
        add_to(tfull.at[c, turn(y, 1), 0, :, :, :, :, cols], yrel.at[0, :, :, :, :, cols])
        y0 = send(tfull.at[c, turn(y, 1), :, :, :, :, :, cols], yin.at[0, :, :, :, :, :, cols], yup)
        r1.wait_recv()
        add_to(tfull.at[c, turn(y, 3), 1, :, :, :, :, cols], yrel.at[1, :, :, :, :, cols])
        y1 = send(tfull.at[c, turn(y, 3), :, :, :, :, :, cols], yin.at[1, :, :, :, :, :, cols], ydown)
        yield
        y0.wait_recv()
        y1.wait_recv()
        xs = []
        for k, (by, target) in enumerate(((2, xpair), (1, xup), (3, xdown), (0, None))):
            h, l = lax.div(turn(x, by), 2), lax.rem(turn(x, by), 2)
            add_to(
                tfull.at[c, y, h, l, :, :, :, cols],
                yin.at[0, h, l, :, :, :, cols],
                yin.at[1, h, l, :, :, :, cols],
            )
            if target is not None:
                xs.append(send(tfull.at[c, y, h, l, :, :, :, cols], xin_t.at[k, :, :, :, cols], target))
        yield
        for copy in xs:
            copy.wait_recv()
        zs = []
        for k, (by, target) in enumerate(((2, zfar), (1, zup), (3, zdown), (0, None))):
            h, l = lax.div(turn(z, by), 2), lax.rem(turn(z, by), 2)
            mine = tfull.at[c, y, xh, xl, h, l, :, cols]
            terms = [xin_t.at[i, h, l, :, cols] for i in range(3)]
            if target is None:
                final = total([mine] + terms)
            else:
                add_to(mine, *terms)
                zs.append(send(mine, zin_t.at[k, :, cols], target))
        yield
        for copy in zs:
            copy.wait_recv()
        final = final + total([zin_t.at[i, :, cols] for i in range(3)])
        for b in range(PIECE // 128):
            block[col // 128 + b] = final[:, b * 128 : (b + 1) * 128]
        sent([s, r0, r1, y0, y1] + xs + zs)
        yield

    def hand_out():
        for r in range(2):
            for b in range(8):
                flat[pl.ds(r * 8 + b, 8, stride=16), :] = block[b, pl.ds(r, 8, stride=2), :]
        copies = []
        for step in range(1, 8):
            j = mate(step)
            copies.append(
                send(flat.at[pl.ds(pl.multiple_of(j * 16, 16), 16), :], gin.at[step], (sec, zh * 8 + j))
            )
        yield
        tgrad_ref[member] = flat[pl.ds(pl.multiple_of(member * 16, 16), 16), :]
        for step, copy in zip(range(1, 8), copies):
            copy.wait_recv()
            tgrad_ref[lax.rem(member + 8 - step, 8)] = gin[step]
        sent(copies)
        yield

    def go(*tasks):
        for task in tasks:
            next(task, None)

    queries[...] = jnp.zeros_like(queries)
    gradout[...] = jnp.zeros_like(gradout)

    tiles = gather_tiles()
    ha = [gather_xz(hfull, part, use_hidden) for part in XZ]
    hb = [gather_zx(hfull, part, use_hidden) for part in ZX]
    ca = [gather_xz(cfull, part, use_cot) for part in XZ]
    cb = [gather_zx(cfull, part, use_cot) for part in ZX]

    go(tiles)
    go(hb[0], ha[0], hb[1], ha[1])
    go(tiles)
    go(*ha)
    go(*hb)
    go(tiles)
    go(cb[0], ca[0], cb[1], ca[1])
    go(*ha)
    go(*hb)
    go(tiles)
    go(*ca)
    go(*hb)
    go(*ha)
    go(*cb)
    go(*ca)
    loads[0].wait()
    go(*hb)
    go(*ha)
    go(tiles)
    go(*cb)
    go(tiles)
    go(*cb)
    go(*ca)
    go(tiles)

    loads[1].wait()
    value = jnp.zeros((ROWS, HD), F32)
    for core in range(2):
        for h in range(2):
            for l in range(2):
                rows = tfull[core, :, h, :, :, l].reshape(ROWS, 1024)
                at = (l * 4 + h * 2 + core) * 1024
                value = value + jnp.dot(rows, wt[pl.ds(at, 1024), :], preferred_element_type=F32)
    proj[...] = value
    normed = value * norm_scale(value) * key_gain
    kv[c] = jnp.where(c == 0, normed, value).astype(BF)
    kv_copy = here(kv.at[c], sib)
    for h in range(HEADS):
        sl = pl.ds(h * HD, HD)
        q = queries[:, sl]
        normedq[:, sl] = (q * norm_scale(q) * query_gain).astype(BF)
    kv_copy.wait_recv()

    keys, values = kv[0], kv[1]
    for h in range(HEADS):
        sl = pl.ds(h * HD, HD)
        scores = contract_last(normedq[:, sl], keys)
        raised = jnp.where(mask[...] > 0.0, jnp.exp(scores), 0.0)
        w = (raised / jnp.sum(raised, axis=-1, keepdims=True)).astype(BF)
        weights[h] = w
        attended[:, sl] = jnp.dot(w, values, preferred_element_type=F32).astype(BF)

    loads[2].wait()
    oa = [scatter_xz(hfull, sib_o, rel_o, zin_o, xin_o, part, make_out, finish_out) for part in XZ]
    ob = [scatter_zx(hfull, sib_o, rel_o, zin_o, xin_o, part, make_out, finish_out) for part in ZX]
    go(ob[0], oa[0], ob[1], oa[1])
    go(*cb)
    go(*ca)
    go(ob[0], oa[0], ob[1], oa[1])

    grad_keys = jnp.zeros((ROWS, HD), F32)
    grad_values = jnp.zeros((ROWS, HD), F32)
    for h in range(HEADS):
        sl = pl.ds(h * HD, HD)
        g = (gate * gradout[:, sl]).astype(BF)
        w = weights[h]
        wide = w.astype(F32)
        prob = contract_last(g, values)
        score = (wide * (prob - jnp.sum(wide * prob, axis=-1, keepdims=True))).astype(BF)
        q = queries[:, sl]
        back = jnp.dot(score, keys, preferred_element_type=F32)
        gradq[:, sl] = head_norm_back(q, norm_scale(q), query_gain, back).astype(BF)
        grad_keys = grad_keys + contract_first(score, normedq[:, sl])
        grad_values = grad_values + contract_first(w, g)
    gxout[...] = jnp.where(c == 0, grad_values, grad_keys).astype(BF)
    gx_copy = send(gxout, gxin, sib)
    kept = jnp.where(c == 0, grad_keys, grad_values).astype(BF).astype(F32)
    go(oa[0], oa[1], ob[0], ob[1])
    gx_copy.wait()
    both = kept + gxin[...].astype(F32)
    raw = proj[...]
    gxout[...] = jnp.where(c == 0, head_norm_back(raw, norm_scale(raw), key_gain, both), both).astype(BF)

    ts = [scatter_tiles(col) for col in range(0, 1024, PIECE)]
    go(*ts)
    ga = [scatter_xz(cfull, sib_g, rel_g, zin_g, xin_g, part, make_grad, finish_grad) for part in XZ]
    gb = [scatter_zx(cfull, sib_g, rel_g, zin_g, xin_g, part, make_grad, finish_grad) for part in ZX]
    go(*ts)
    go(gb[0], ga[0], gb[1], ga[1])
    go(*ob)
    go(*oa)
    go(*ts)
    go(gb[0], ga[0], gb[1], ga[1])
    go(*ob)
    go(*oa)
    go(*ga)
    go(*gb)
    go(*ts)
    go(*ga)
    go(*gb)
    go(*ts)
    go(*ga)
    go(*gb)
    go(*ts)
    last = hand_out()
    go(last)
    go(last)
    kv_copy.wait_send()


def body(hidden, tiles, tile_counts, sample_order, query_weight, tile_weight, output_weight, head_gains, cross_gate, cotangent):
    til = tiles.reshape(2, 8, 8, 128).transpose(1, 0, 2, 3).reshape(8, 16, 128)
    smem = pl.BlockSpec(memory_space=pltpu.SMEM)
    vmem = pl.BlockSpec(memory_space=pltpu.VMEM)
    hbm = pl.BlockSpec(memory_space=pl.ANY)
    rows = (2, 4, 2, 16, D)

    def tp_buffers():
        return [
            pltpu.VMEM((4, 2, 16, D), BF),
            pltpu.VMEM((2, 2, 16, D), BF),
            pltpu.VMEM((2, 2, 16, D), BF),
            pltpu.VMEM((4, 16, D), BF),
        ]

    copies = 200
    out, grad, tgrad = pl.pallas_call(
        kernel,
        out_shape=(
            jax.ShapeDtypeStruct((16, D), BF),
            jax.ShapeDtypeStruct((16, D), BF),
            jax.ShapeDtypeStruct((8, 16, 128), F32),
        ),
        in_specs=[smem, smem, smem, vmem, vmem, vmem, vmem, hbm, hbm, hbm],
        out_specs=(vmem, vmem, vmem),
        scratch_shapes=[
            pltpu.VMEM((D, LOCAL), BF),
            pltpu.VMEM((D, HD), BF),
            pltpu.VMEM((LOCAL, D), BF),
            pltpu.VMEM(rows, BF),
            pltpu.VMEM(rows, BF),
            pltpu.VMEM((2, 4, 2, 2, 2, 2, 16, 1024), BF),
            *tp_buffers(),
            *tp_buffers(),
            pltpu.VMEM((4, 2, 2, 2, 2, 16, 1024), BF),
            pltpu.VMEM((2, 2, 2, 2, 16, 1024), BF),
            pltpu.VMEM((2, 2, 2, 2, 2, 16, 1024), BF),
            pltpu.VMEM((3, 2, 2, 16, 1024), BF),
            pltpu.VMEM((3, 16, 1024), BF),
            pltpu.VMEM((8, 16, 128), BF),
            pltpu.VMEM((128, 128), F32),
            pltpu.VMEM((8, 16, 128), F32),
            pltpu.VMEM((8, 16, 128), F32),
            pltpu.VMEM((ROWS, LOCAL), F32),
            pltpu.VMEM((ROWS, LOCAL), F32),
            pltpu.VMEM((ROWS, LOCAL), BF),
            pltpu.VMEM((HEADS, ROWS, ROWS), BF),
            pltpu.VMEM((ROWS, LOCAL), BF),
            pltpu.VMEM((ROWS, LOCAL), BF),
            pltpu.VMEM((ROWS, HD), F32),
            pltpu.VMEM((2, ROWS, HD), BF),
            pltpu.VMEM((ROWS, HD), BF),
            pltpu.VMEM((ROWS, HD), BF),
            pltpu.VMEM((ROWS, ROWS), F32),
            pltpu.SemaphoreType.DMA((3,)),
            pltpu.SemaphoreType.DMA((copies,)),
            pltpu.SemaphoreType.DMA((copies,)),
        ],
        compiler_params=pltpu.CompilerParams(
            collective_id=0, has_side_effects=True, vmem_limit_bytes=60 * 2**20
        ),
        name="cross_attention",
    )(
        tile_counts, sample_order, cross_gate, head_gains[0], hidden[0], cotangent[0], til,
        query_weight[0], tile_weight[0], output_weight[0],
    )
    tile_grad = tgrad.reshape(8, 2, 8, 128).transpose(1, 0, 2, 3).reshape(2, D)
    return (out[None], grad[None], tile_grad)


def solution(mesh):
    placed = (
        P("section", "tp", None),
        P(("section", "tp"), None),
        P(),
        P(),
        P("section", None, "tp"),
        P("section", None, "tp"),
        P("section", "tp", None),
        P("section", None, None),
        P("section"),
        P("section", "tp", None),
    )
    return jax.shard_map(
        body,
        mesh=mesh,
        in_specs=placed,
        out_specs=(P("section", "tp", None), P("section", "tp", None), P(("section", "tp"), None)),
        check_vma=False,
    )
```

```python
import functools
import jax
import jax.numpy as jnp
from jax import lax
from jax.experimental import pallas as pl
from jax.experimental.pallas import tpu as pltpu
from jax.sharding import PartitionSpec as P

MESH = pl.DeviceIdType.MESH
NORM_EPS = 1e-06
D = 8192
HD = 128
LOCAL = 512
HEADS = 4
ROWS = 256
BF = jnp.bfloat16
F32 = jnp.float32

XZ = ((0, 2560), (2560, 2560))
ZX = ((5120, 1536), (6656, 1536))
PIECE = 512

ORDER = (
    "ca0", "ha0", "ha1", "t", "hb0", "hb0", "ca1", "cb1", "cb1", "cb0", "hb1", "hb1", "cb0", "t",
    "ca0", "hb0", "cb1", "ha0", "cb0", "hb1", "ha1", "t", "ca1", "ca0", "hb0", "cb1", "ha0", "cb0",
    "hb1", "ha1", "t", "t", "ca1", "ca0", "t", "t", "ha0", "hb0", "ca0", "t", "cb1", "ha1", "cb0",
    "ha0", "hb0", "ca1", "hb1", "t", "cb1", "ha1", "t", "cb0", "ca1", "hb1", "t", "t", "t", "bw",
    "gb0", "oa1", "oa0", "gb0", "bw", "p1", "oa1", "ob1", "p0", "oa0", "ob0", "p1", "ob1", "oa1",
    "ga1", "gb0", "p0", "oa0", "ob0", "ga0", "ga1", "p1", "gb1", "oa1", "gb0", "ob1", "ga0", "p0",
    "gb1", "oa0", "ob0", "ga1", "oa1", "gb0", "p1", "ob1", "ga0", "ob0", "gb1", "p0", "ga1", "oa0",
    "ob1", "p1", "ga0", "p0", "ob0", "gb1", "ga1", "p1", "p0", "l", "ga0", "gb1", "l",
)


def contract_last(left, right):
    return lax.dot_general(left, right, (((1,), (1,)), ((), ())), preferred_element_type=F32)


def contract_first(left, right):
    return lax.dot_general(left, right, (((0,), (0,)), ((), ())), preferred_element_type=F32)


def norm_scale(values):
    return lax.rsqrt(jnp.mean(values * values, axis=-1, keepdims=True) + NORM_EPS)


def head_norm_back(values, scale, gain, grad):
    normed = values * scale
    scaled = grad * gain
    return scale * (scaled - normed * jnp.mean(normed * scaled, axis=-1, keepdims=True))


def add_to(total, *terms):
    value = total[...].astype(F32)
    for term in terms:
        value = value + term[...].astype(F32)
    total[...] = value.astype(total.dtype)


def kernel(
    counts, order, gate_ref, gains, hid, cot, tiles_ref, wq_hbm, wt_hbm, wo_hbm,
    out_ref, grad_ref, tgrad_ref,
    wq, wt, wo, hfull, cfull, tfull,
    sib_o, rel_o, zin_o, xin_o,
    sib_g, rel_g, zin_g, xin_g,
    sib_t, yrel, yin, xin_t, zin_t,
    til, tin, flat, block, gin,
    queries, gradout, normedq, weights, attended, gradq, proj, kv, gxin, gxout, mask,
    load_sem, send_sem, recv_sem,
):
    sec = lax.axis_index("section")
    tp = lax.axis_index("tp")
    y, xl = lax.div(sec, 2), lax.rem(sec, 2)
    z, xh, c = lax.div(tp, 4), lax.rem(lax.div(tp, 2), 2), lax.rem(tp, 2)
    x = xh * 2 + xl
    zh, zl = lax.div(z, 2), lax.rem(z, 2)
    member = lax.rem(tp, 8)
    oc, ox = 1 - c, 1 - xh

    def turn(value, by):
        return lax.rem(value + by, 4)

    def device(dx=0, dy=0, dz=0, core=None):
        nx, ny, nz = turn(x, dx), turn(y, dy), turn(z, dz)
        core = c if core is None else core
        return (ny * 2 + lax.rem(nx, 2), nz * 4 + lax.div(nx, 2) * 2 + core)

    def mate(step):
        return lax.rem(member + step, 8)

    sib = device(core=oc)
    xpair = device(dx=2)
    zup, zdown, zfar = device(dz=1), device(dz=3), device(dz=2)
    yup, ydown = device(dy=1), device(dy=3)
    xup, xdown = device(dx=1), device(dx=3)

    loads = []
    for i, (src, dst) in enumerate(((wq_hbm, wq), (wt_hbm, wt), (wo_hbm, wo))):
        loads.append(pltpu.make_async_copy(src, dst, load_sem.at[i]))
        loads[-1].start()

    barrier = pltpu.get_barrier_semaphore()
    zodd = device(dz=lax.rem(zl * 2 + 3, 4))
    greeted = [(sec, zh * 8 + mate(step)) for step in range(1, 8)]
    greeted += [zodd, zfar, yup, ydown, xup, xdown]
    for other in greeted:
        pl.semaphore_signal(barrier, inc=1, device_id=other, device_id_type=MESH)

    hfull[c, z, xh] = hid[...]
    cfull[c, z, xh] = cot[...]

    tile_index = lax.div(lax.broadcasted_iota(jnp.int32, (1, ROWS), 1), 32)
    tile_sample = jnp.zeros((1, ROWS), jnp.int32)
    end = jnp.int32(0)
    for i in range(4):
        end = end + counts[i]
        tile_sample = tile_sample + (tile_index >= end).astype(jnp.int32)
    for i in range(4):
        row = (tile_sample == order[i]).astype(F32)
        for half in range(2):
            mask[pl.ds(half * 128 + i * 32, 32), :] = jnp.broadcast_to(row, (32, ROWS))
    gate = jnp.tanh(jnp.full((1, HD), gate_ref[0], F32))
    query_gain = gains[0:1, :] * HD ** (-0.5)
    key_gain = gains[1:2, :]

    pl.semaphore_wait(barrier, len(greeted))

    used = [0]

    def send(src, dst, target):
        i = used[0]
        used[0] += 1
        copy = pltpu.make_async_remote_copy(
            src_ref=src, dst_ref=dst, send_sem=send_sem.at[i], recv_sem=recv_sem.at[i],
            device_id=target, device_id_type=MESH,
        )
        copy.start()
        return copy

    def here(ref, target):
        return send(ref, ref, target)

    def sent(copies):
        for copy in copies:
            copy.wait_send()

    def gather_xz(full, part, use):
        col, width = part
        cols = pl.ds(col, width)
        low, high = pl.ds(col, width // 2), pl.ds(col + width // 2, width // 2)
        a = here(full.at[c, z, xh, :, cols], xpair)
        yield
        a.wait_recv()
        up = here(full.at[c, z, :, :, cols], zup)
        down = here(full.at[c, z, :, :, cols], zdown)
        yield
        up.wait_recv()
        up2 = here(full.at[c, turn(z, 3), :, :, low], zup)
        down.wait_recv()
        down2 = here(full.at[c, turn(z, 1), :, :, high], zdown)
        yield
        up2.wait_recv()
        down2.wait_recv()
        s = here(full.at[c, :, :, :, cols], sib)
        yield
        s.wait_recv()
        use(part)
        sent([a, up, down, up2, down2, s])
        yield

    def gather_zx(full, part, use):
        col, width = part
        cols = pl.ds(col, width)
        low, high = pl.ds(col, width // 2), pl.ds(col + width // 2, width // 2)
        mine = full.at[c, z, xh, :, cols]
        up, down = here(mine, zup), here(mine, zdown)
        yield
        a = here(mine, xpair)
        yield
        up.wait_recv()
        up2 = here(full.at[c, turn(z, 3), xh, :, low], zup)
        a1 = here(full.at[c, turn(z, 3), xh, :, cols], xpair)
        down.wait_recv()
        down2 = here(full.at[c, turn(z, 1), xh, :, high], zdown)
        a2 = here(full.at[c, turn(z, 1), xh, :, cols], xpair)
        yield
        up2.wait_recv()
        down2.wait_recv()
        a3 = here(full.at[c, turn(z, 2), xh, :, cols], xpair)
        yield
        for copy in (a, a1, a2, a3):
            copy.wait_recv()
        s = here(full.at[c, :, :, :, cols], sib)
        yield
        s.wait_recv()
        use(part)
        sent([up, down, a, up2, a1, down2, a2, a3, s])
        yield

    loaded = set()

    def need(i):
        if i not in loaded:
            loaded.add(i)
            loads[i].wait()

    def use_hidden(part):
        need(0)
        at = pl.ds(*part)
        rows = hfull[:, :, :, :, at].reshape(ROWS, part[1])
        queries[...] += jnp.dot(rows, wq[at, :], preferred_element_type=F32)

    def use_cot(part):
        need(2)
        at = pl.ds(*part)
        rows = cfull[:, :, :, :, at].reshape(ROWS, part[1])
        gradout[...] += contract_last(rows, wo[:, at])

    def tblock(full, yy, xx):
        return full.at[c, yy, lax.div(xx, 2), lax.rem(xx, 2)]

    def gather_tiles():
        wide = tiles_ref[...].astype(F32)
        for j in range(8):
            for b in range(8):
                at = (j * 8 + b) * 128
                flat[pl.ds(j * 16 + b, 2, stride=8), :] = wide[:, at : at + 128]
        for j in range(8):
            til[j] = flat[j * 16 : (j + 1) * 16, :].astype(BF)
        copies = []
        for step in range(1, 8):
            j = mate(step)
            copies.append(send(til.at[j], tin.at[step], (sec, zh * 8 + j)))
        yield
        for copy in copies:
            copy.wait_recv()
        tin[0] = til[member]
        for s in range(8):
            owner = lax.rem(member + 8 - s, 8)
            flat[pl.ds(pl.multiple_of(owner * 16, 16), 16), :] = tin[s].astype(F32)
        for r in range(2):
            for b in range(8):
                block[b, pl.ds(r, 8, stride=2), :] = flat[pl.ds(r * 8 + b, 8, stride=16), :]
        own = tfull.at[c, y, xh, xl, zh, zl]
        for b in range(8):
            own[:, pl.ds(b * 128, 128)] = block[b].astype(BF)
        zs = [here(own, zup), here(own, zdown), here(own, zfar)]
        yield
        for copy in zs:
            copy.wait_recv()
        mine = tblock(tfull, y, x)
        xs = [here(mine, xup), here(mine, xdown), here(mine, xpair)]
        ups, downs = [here(mine, yup)], [here(mine, ydown)]
        for copy, by in zip(xs, (3, 1, 2)):
            yield
            copy.wait_recv()
            got = tblock(tfull, y, turn(x, by))
            ups.append(here(got, yup))
            downs.append(here(got, ydown))
        sibs = [here(tfull.at[c, y], sib)]
        far = []
        for k, by in enumerate((0, 3, 1, 2)):
            yield
            ups[k].wait_recv()
            downs[k].wait_recv()
            if k % 2 == 0:
                far.append(here(tblock(tfull, turn(y, 3), turn(x, by)), yup))
            else:
                far.append(here(tblock(tfull, turn(y, 1), turn(x, by)), ydown))
        sibs.append(here(tfull.at[c, turn(y, 3)], sib))
        sibs.append(here(tfull.at[c, turn(y, 1)], sib))
        yield
        for copy in far:
            copy.wait_recv()
        sibs.append(here(tfull.at[c, turn(y, 2)], sib))
        yield
        for copy in sibs:
            copy.wait_recv()
        sent(copies + zs + xs + ups + downs + far + sibs)
        yield from attend()
        yield

    def scatter_xz(full, sibin, rel, zin, xin, part, make, finish):
        col, width = part
        cols = pl.ds(col, width)
        low, high = pl.ds(col, width // 2), pl.ds(col + width // 2, width // 2)
        make(part)
        s = send(full.at[oc, :, :, :, cols], sibin.at[:, :, :, cols], sib)
        yield
        s.wait_recv()
        add_to(full.at[c, turn(z, 2), :, :, cols], sibin.at[turn(z, 2), :, :, cols])
        r0 = send(full.at[c, turn(z, 2), :, :, low], rel.at[0, :, :, low], zup)
        r1 = send(full.at[c, turn(z, 2), :, :, high], rel.at[1, :, :, high], zdown)
        for by in (1, 3, 0):
            add_to(full.at[c, turn(z, by), :, :, cols], sibin.at[turn(z, by), :, :, cols])
        yield
        r0.wait_recv()
        add_to(full.at[c, turn(z, 1), :, :, low], rel.at[0, :, :, low])
        z0 = send(full.at[c, turn(z, 1), :, :, cols], zin.at[0, :, :, cols], zup)
        r1.wait_recv()
        add_to(full.at[c, turn(z, 3), :, :, high], rel.at[1, :, :, high])
        z1 = send(full.at[c, turn(z, 3), :, :, cols], zin.at[1, :, :, cols], zdown)
        yield
        z0.wait_recv()
        z1.wait_recv()
        add_to(full.at[c, z, ox, :, cols], zin.at[0, ox, :, cols], zin.at[1, ox, :, cols])
        a = send(full.at[c, z, ox, :, cols], xin.at[0, :, cols], xpair)
        yield
        a.wait_recv()
        finish(cols, (full.at[c, z, xh, :, cols], zin.at[0, xh, :, cols], zin.at[1, xh, :, cols], xin.at[0, :, cols]))
        sent([s, r0, r1, z0, z1, a])
        yield

    def scatter_zx(full, sibin, rel, zin, xin, part, make, finish):
        col, width = part
        cols = pl.ds(col, width)
        low, high = pl.ds(col, width // 2), pl.ds(col + width // 2, width // 2)
        make(part)
        s = send(full.at[oc, :, :, :, cols], sibin.at[:, :, :, cols], sib)
        yield
        s.wait_recv()
        add_to(full.at[c, :, ox, :, cols], sibin.at[:, ox, :, cols])
        a = send(full.at[c, :, ox, :, cols], xin.at[:, :, cols], xpair)
        yield
        a.wait_recv()
        add_to(full.at[c, turn(z, 2), xh, :, cols], sibin.at[turn(z, 2), xh, :, cols], xin.at[turn(z, 2), :, cols])
        r0 = send(full.at[c, turn(z, 2), xh, :, low], rel.at[0, 0, :, low], zup)
        r1 = send(full.at[c, turn(z, 2), xh, :, high], rel.at[1, 0, :, high], zdown)
        for by in (1, 3):
            add_to(full.at[c, turn(z, by), xh, :, cols], sibin.at[turn(z, by), xh, :, cols], xin.at[turn(z, by), :, cols])
        yield
        r0.wait_recv()
        add_to(full.at[c, turn(z, 1), xh, :, low], rel.at[0, 0, :, low])
        z0 = send(full.at[c, turn(z, 1), xh, :, cols], zin.at[0, 0, :, cols], zup)
        r1.wait_recv()
        add_to(full.at[c, turn(z, 3), xh, :, high], rel.at[1, 0, :, high])
        z1 = send(full.at[c, turn(z, 3), xh, :, cols], zin.at[1, 0, :, cols], zdown)
        yield
        z0.wait_recv()
        z1.wait_recv()
        finish(cols, (full.at[c, z, xh, :, cols], sibin.at[z, xh, :, cols], xin.at[z, :, cols], zin.at[0, 0, :, cols], zin.at[1, 0, :, cols]))
        sent([s, a, r0, r1, z0, z1])
        yield

    def total(terms):
        value = terms[0][...].astype(F32)
        for term in terms[1:]:
            value = value + term[...].astype(F32)
        return value

    def make_out(part):
        at = pl.ds(*part)
        value = jnp.dot(attended[...], wo[:, at], preferred_element_type=F32)
        hfull[:, :, :, :, at] = value.astype(BF).reshape(2, 4, 2, 16, part[1])

    def finish_out(cols, terms):
        out_ref[:, cols] = (hid[:, cols].astype(F32) + gate[0:1, 0:1] * total(terms)).astype(BF)

    def make_grad(part):
        at = pl.ds(*part)
        value = contract_last(gradq[...], wq[at, :])
        cfull[:, :, :, :, at] = value.astype(BF).reshape(2, 4, 2, 16, part[1])

    def finish_grad(cols, terms):
        grad_ref[:, cols] = (cot[:, cols].astype(F32) + total(terms)).astype(BF)

    def scatter_tiles(col):
        cols = pl.ds(col, PIECE)

        def unit(ref, *index):
            return ref.at[(*index, Ellipsis, cols)]

        for core in (oc, c):
            for h in range(2):
                for l in range(2):
                    at = (l * 4 + h * 2 + core) * 1024 + col
                    value = contract_last(gxout[...], wt[pl.ds(pl.multiple_of(at, 128), PIECE), :])
                    tfull[core, :, h, :, :, l, :, cols] = value.astype(BF).reshape(4, 2, 2, 16, PIECE)
            if core is oc:
                s = send(tfull.at[oc, :, :, :, :, :, :, cols], sib_t.at[:, :, :, :, :, :, cols], sib)
        yield
        s.wait_recv()

        def merge(by):
            yy = turn(y, by)
            for h in range(2):
                add_to(tfull.at[c, yy, h, :, :, :, :, cols], sib_t.at[yy, h, :, :, :, :, cols])

        merge(2)
        r0 = send(tfull.at[c, turn(y, 2), 0, :, :, :, :, cols], yrel.at[0, :, :, :, :, cols], yup)
        r1 = send(tfull.at[c, turn(y, 2), 1, :, :, :, :, cols], yrel.at[1, :, :, :, :, cols], ydown)
        for by in (1, 3, 0):
            merge(by)
        yield
        r0.wait_recv()
        add_to(tfull.at[c, turn(y, 1), 0, :, :, :, :, cols], yrel.at[0, :, :, :, :, cols])
        y0 = send(tfull.at[c, turn(y, 1), :, :, :, :, :, cols], yin.at[0, :, :, :, :, :, cols], yup)
        r1.wait_recv()
        add_to(tfull.at[c, turn(y, 3), 1, :, :, :, :, cols], yrel.at[1, :, :, :, :, cols])
        y1 = send(tfull.at[c, turn(y, 3), :, :, :, :, :, cols], yin.at[1, :, :, :, :, :, cols], ydown)
        yield
        y0.wait_recv()
        y1.wait_recv()
        xs = []
        for k, (by, target) in enumerate(((2, xpair), (1, xup), (3, xdown), (0, None))):
            h, l = lax.div(turn(x, by), 2), lax.rem(turn(x, by), 2)
            add_to(
                tfull.at[c, y, h, l, :, :, :, cols],
                yin.at[0, h, l, :, :, :, cols],
                yin.at[1, h, l, :, :, :, cols],
            )
            if target is not None:
                xs.append(send(tfull.at[c, y, h, l, :, :, :, cols], xin_t.at[k, :, :, :, cols], target))
        yield
        for copy in xs:
            copy.wait_recv()
        zs = []
        for k, (by, target) in enumerate(((2, zfar), (1, zup), (3, zdown), (0, None))):
            h, l = lax.div(turn(z, by), 2), lax.rem(turn(z, by), 2)
            mine = tfull.at[c, y, xh, xl, h, l, :, cols]
            terms = [xin_t.at[i, h, l, :, cols] for i in range(3)]
            if target is None:
                final = total([mine] + terms)
            else:
                add_to(mine, *terms)
                zs.append(send(mine, zin_t.at[k, :, cols], target))
        yield
        for copy in zs:
            copy.wait_recv()
        final = final + total([zin_t.at[i, :, cols] for i in range(3)])
        for b in range(PIECE // 128):
            block[col // 128 + b] = final[:, b * 128 : (b + 1) * 128]
        sent([s, r0, r1, y0, y1] + xs + zs)
        yield

    def hand_out():
        for r in range(2):
            for b in range(8):
                flat[pl.ds(r * 8 + b, 8, stride=16), :] = block[b, pl.ds(r, 8, stride=2), :]
        copies = []
        for step in range(1, 8):
            j = mate(step)
            copies.append(
                send(flat.at[pl.ds(pl.multiple_of(j * 16, 16), 16), :], gin.at[step], (sec, zh * 8 + j))
            )
        yield
        gin[0] = flat[pl.ds(pl.multiple_of(member * 16, 16), 16), :]
        for copy in copies:
            copy.wait_recv()
        sent(copies)
        for s in range(8):
            owner = lax.rem(member + 8 - s, 8)
            flat[pl.ds(pl.multiple_of(owner * 16, 16), 16), :] = gin[s]
        for j in range(8):
            for b in range(8):
                tgrad_ref[:, pl.ds((j * 8 + b) * 128, 128)] = flat[pl.ds(j * 16 + b, 2, stride=8), :]
        yield

    def attend():
        need(1)
        value = jnp.zeros((ROWS, HD), F32)
        for core in range(2):
            for h in range(2):
                for l in range(2):
                    rows = tfull[core, :, h, :, :, l].reshape(ROWS, 1024)
                    at = (l * 4 + h * 2 + core) * 1024
                    value = value + jnp.dot(rows, wt[pl.ds(at, 1024), :], preferred_element_type=F32)
        proj[...] = value
        normed = value * norm_scale(value) * key_gain
        kv[c] = jnp.where(c == 0, normed, value).astype(BF)
        kv_copy = here(kv.at[c], sib)
        yield
        for h in range(HEADS):
            sl = pl.ds(h * HD, HD)
            q = queries[:, sl]
            normedq[:, sl] = (q * norm_scale(q) * query_gain).astype(BF)
        kv_copy.wait_recv()

        keys, values = kv[0], kv[1]
        for h in range(HEADS):
            sl = pl.ds(h * HD, HD)
            scores = contract_last(normedq[:, sl], keys)
            raised = jnp.where(mask[...] > 0.0, jnp.exp(scores), 0.0)
            w = (raised / jnp.sum(raised, axis=-1, keepdims=True)).astype(BF)
            weights[h] = w
            attended[:, sl] = jnp.dot(w, values, preferred_element_type=F32).astype(BF)
        kv_copy.wait_send()

    def attend_back():
        keys, values = kv[0], kv[1]
        grad_keys = jnp.zeros((ROWS, HD), F32)
        grad_values = jnp.zeros((ROWS, HD), F32)
        for h in range(HEADS):
            sl = pl.ds(h * HD, HD)
            g = (gate * gradout[:, sl]).astype(BF)
            w = weights[h]
            wide = w.astype(F32)
            prob = contract_last(g, values)
            score = (wide * (prob - jnp.sum(wide * prob, axis=-1, keepdims=True))).astype(BF)
            q = queries[:, sl]
            back = jnp.dot(score, keys, preferred_element_type=F32)
            gradq[:, sl] = head_norm_back(q, norm_scale(q), query_gain, back).astype(BF)
            grad_keys = grad_keys + contract_first(score, normedq[:, sl])
            grad_values = grad_values + contract_first(w, g)
        gxout[...] = jnp.where(c == 0, grad_values, grad_keys).astype(BF)
        gx_copy = send(gxout, gxin, sib)
        kept = jnp.where(c == 0, grad_keys, grad_values).astype(BF).astype(F32)
        yield
        gx_copy.wait()
        both = kept + gxin[...].astype(F32)
        raw = proj[...]
        gxout[...] = jnp.where(c == 0, head_norm_back(raw, norm_scale(raw), key_gain, both), both).astype(BF)
        yield

    queries[...] = jnp.zeros_like(queries)
    gradout[...] = jnp.zeros_like(gradout)

    tasks = {"t": gather_tiles(), "bw": attend_back(), "l": hand_out()}
    for i in range(2):
        tasks["ha%d" % i] = gather_xz(hfull, XZ[i], use_hidden)
        tasks["hb%d" % i] = gather_zx(hfull, ZX[i], use_hidden)
        tasks["ca%d" % i] = gather_xz(cfull, XZ[i], use_cot)
        tasks["cb%d" % i] = gather_zx(cfull, ZX[i], use_cot)
        tasks["oa%d" % i] = scatter_xz(hfull, sib_o, rel_o, zin_o, xin_o, XZ[i], make_out, finish_out)
        tasks["ob%d" % i] = scatter_zx(hfull, sib_o, rel_o, zin_o, xin_o, ZX[i], make_out, finish_out)
        tasks["ga%d" % i] = scatter_xz(cfull, sib_g, rel_g, zin_g, xin_g, XZ[i], make_grad, finish_grad)
        tasks["gb%d" % i] = scatter_zx(cfull, sib_g, rel_g, zin_g, xin_g, ZX[i], make_grad, finish_grad)
    for i in range(1024 // PIECE):
        tasks["p%d" % i] = scatter_tiles(i * PIECE)
    for name in ORDER:
        next(tasks[name])


def body(hidden, tiles, tile_counts, sample_order, query_weight, tile_weight, output_weight, head_gains, cross_gate, cotangent):
    smem = pl.BlockSpec(memory_space=pltpu.SMEM)
    vmem = pl.BlockSpec(memory_space=pltpu.VMEM)
    hbm = pl.BlockSpec(memory_space=pl.ANY)
    rows = (2, 4, 2, 16, D)

    def tp_buffers():
        return [
            pltpu.VMEM((4, 2, 16, D), BF),
            pltpu.VMEM((2, 2, 16, D), BF),
            pltpu.VMEM((2, 2, 16, D), BF),
            pltpu.VMEM((4, 16, D), BF),
        ]

    copies = 200
    out, grad, tgrad = pl.pallas_call(
        kernel,
        out_shape=(
            jax.ShapeDtypeStruct((16, D), BF),
            jax.ShapeDtypeStruct((16, D), BF),
            jax.ShapeDtypeStruct((2, D), F32),
        ),
        in_specs=[smem, smem, smem, vmem, vmem, vmem, vmem, hbm, hbm, hbm],
        out_specs=(vmem, vmem, vmem),
        scratch_shapes=[
            pltpu.VMEM((D, LOCAL), BF),
            pltpu.VMEM((D, HD), BF),
            pltpu.VMEM((LOCAL, D), BF),
            pltpu.VMEM(rows, BF),
            pltpu.VMEM(rows, BF),
            pltpu.VMEM((2, 4, 2, 2, 2, 2, 16, 1024), BF),
            *tp_buffers(),
            *tp_buffers(),
            pltpu.VMEM((4, 2, 2, 2, 2, 16, 1024), BF),
            pltpu.VMEM((2, 2, 2, 2, 16, 1024), BF),
            pltpu.VMEM((2, 2, 2, 2, 2, 16, 1024), BF),
            pltpu.VMEM((3, 2, 2, 16, 1024), BF),
            pltpu.VMEM((3, 16, 1024), BF),
            pltpu.VMEM((8, 16, 128), BF),
            pltpu.VMEM((8, 16, 128), BF),
            pltpu.VMEM((128, 128), F32),
            pltpu.VMEM((8, 16, 128), F32),
            pltpu.VMEM((8, 16, 128), F32),
            pltpu.VMEM((ROWS, LOCAL), F32),
            pltpu.VMEM((ROWS, LOCAL), F32),
            pltpu.VMEM((ROWS, LOCAL), BF),
            pltpu.VMEM((HEADS, ROWS, ROWS), BF),
            pltpu.VMEM((ROWS, LOCAL), BF),
            pltpu.VMEM((ROWS, LOCAL), BF),
            pltpu.VMEM((ROWS, HD), F32),
            pltpu.VMEM((2, ROWS, HD), BF),
            pltpu.VMEM((ROWS, HD), BF),
            pltpu.VMEM((ROWS, HD), BF),
            pltpu.VMEM((ROWS, ROWS), F32),
            pltpu.SemaphoreType.DMA((3,)),
            pltpu.SemaphoreType.DMA((copies,)),
            pltpu.SemaphoreType.DMA((copies,)),
        ],
        compiler_params=pltpu.CompilerParams(
            collective_id=0, has_side_effects=True, vmem_limit_bytes=60 * 2**20
        ),
        name="cross_attention",
    )(
        tile_counts, sample_order, cross_gate, head_gains[0], hidden[0], cotangent[0], tiles,
        query_weight[0], tile_weight[0], output_weight[0],
    )
    return (out[None], grad[None], tgrad)


def solution(mesh):
    placed = (
        P("section", "tp", None),
        P(("section", "tp"), None),
        P(),
        P(),
        P("section", None, "tp"),
        P("section", None, "tp"),
        P("section", "tp", None),
        P("section", None, None),
        P("section"),
        P("section", "tp", None),
    )
    return jax.shard_map(
        body,
        mesh=mesh,
        in_specs=placed,
        out_specs=(P("section", "tp", None), P("section", "tp", None), P(("section", "tp"), None)),
        check_vma=False,
    )
```

```python
import functools
import jax
import jax.numpy as jnp
from jax import lax
from jax.experimental import pallas as pl
from jax.experimental.pallas import tpu as pltpu
from jax.sharding import PartitionSpec as P

MESH = pl.DeviceIdType.MESH
NORM_EPS = 1e-06
D = 8192
HD = 128
LOCAL = 512
HEADS = 4
ROWS = 256
BF = jnp.bfloat16
F32 = jnp.float32

XZ = ((0, 2560), (2560, 2560))
ZX = ((5120, 1536), (6656, 1536))
PIECE = 256

ORDER = (
    "t", "ca1", "ca0", "cb0", "hb0", "t", "ha1", "cb0", "cb1", "ca1", "hb0", "t", "hb0", "ca0",
    "ha1", "hb0", "t", "ca1", "ha0", "t", "cb0", "ca0", "t", "cb1", "hb1", "t", "hb0", "cb1", "t",
    "ca1", "ha0", "ca0", "hb0", "t", "hb1", "cb0", "t", "cb1", "hb1", "ha1", "ca0", "ha0", "hb1",
    "ca1", "cb0", "cb1", "ha1", "t", "ha0", "cb0", "cb1", "hb1", "ha1", "t", "ha0", "hb1", "t",
    "ob1", "bw", "oa0", "ga0", "gb0", "ob1", "bw", "d", "oa0", "ga1", "ga0", "d", "p0", "gb1", "p1",
    "gb0", "oa0", "ob0", "p3", "ob1", "oa1", "p2", "ob0", "ga1", "gb1", "p0", "oa1", "p3", "p1",
    "gb0", "ob1", "ga1", "p0", "p2", "oa1", "oa0", "ob0", "p3", "p0", "gb1", "ga0", "p1", "p2",
    "ob1", "ob0", "ga1", "oa1", "p3", "p1", "oa0", "p2", "gb1", "gb0", "ga0", "ga1", "p0", "p3",
    "p1", "p2", "l", "ob0", "oa1", "gb0", "gb1", "ga0", "l",
)


def contract_last(left, right):
    return lax.dot_general(left, right, (((1,), (1,)), ((), ())), preferred_element_type=F32)


def contract_first(left, right):
    return lax.dot_general(left, right, (((0,), (0,)), ((), ())), preferred_element_type=F32)


def norm_scale(values):
    return lax.rsqrt(jnp.mean(values * values, axis=-1, keepdims=True) + NORM_EPS)


def head_norm_back(values, scale, gain, grad):
    normed = values * scale
    scaled = grad * gain
    return scale * (scaled - normed * jnp.mean(normed * scaled, axis=-1, keepdims=True))


def add_to(total, *terms):
    value = total[...].astype(F32)
    for term in terms:
        value = value + term[...].astype(F32)
    total[...] = value.astype(total.dtype)


def kernel(
    counts, order, gate_ref, gains, hid, cot, tiles_ref, wq_hbm, wt_hbm, wo_hbm,
    out_ref, grad_ref, tgrad_ref,
    wq, wt, wo, hfull, cfull, tfull,
    sib_o, rel_o, zin_o, xin_o,
    sib_g, rel_g, zin_g, xin_g,
    sib_t, yrel, yin, xin_t, zin_t,
    til, tin, flat, block, gin,
    queries, gradout, normedq, weights, attended, gradq, proj, kv, gxin, gxout, mask,
    load_sem, send_sem, recv_sem,
):
    sec = lax.axis_index("section")
    tp = lax.axis_index("tp")
    y, xl = lax.div(sec, 2), lax.rem(sec, 2)
    z, xh, c = lax.div(tp, 4), lax.rem(lax.div(tp, 2), 2), lax.rem(tp, 2)
    x = xh * 2 + xl
    zh, zl = lax.div(z, 2), lax.rem(z, 2)
    member = lax.rem(tp, 8)
    oc, ox = 1 - c, 1 - xh

    def turn(value, by):
        return lax.rem(value + by, 4)

    def device(dx=0, dy=0, dz=0, core=None):
        nx, ny, nz = turn(x, dx), turn(y, dy), turn(z, dz)
        core = c if core is None else core
        return (ny * 2 + lax.rem(nx, 2), nz * 4 + lax.div(nx, 2) * 2 + core)

    def mate(step):
        return lax.rem(member + step, 8)

    sib = device(core=oc)
    xpair = device(dx=2)
    zup, zdown, zfar = device(dz=1), device(dz=3), device(dz=2)
    yup, ydown = device(dy=1), device(dy=3)
    xup, xdown = device(dx=1), device(dx=3)

    loads = []
    for i, (src, dst) in enumerate(((wq_hbm, wq), (wt_hbm, wt), (wo_hbm, wo))):
        loads.append(pltpu.make_async_copy(src, dst, load_sem.at[i]))
        loads[-1].start()

    barrier = pltpu.get_barrier_semaphore()
    zodd = device(dz=lax.rem(zl * 2 + 3, 4))
    greeted = [(sec, zh * 8 + mate(step)) for step in range(1, 8)]
    greeted += [zodd, zfar, yup, ydown, xup, xdown]
    for other in greeted:
        pl.semaphore_signal(barrier, inc=1, device_id=other, device_id_type=MESH)

    hfull[c, z, xh] = hid[...]
    cfull[c, z, xh] = cot[...]

    tile_index = lax.div(lax.broadcasted_iota(jnp.int32, (1, ROWS), 1), 32)
    tile_sample = jnp.zeros((1, ROWS), jnp.int32)
    end = jnp.int32(0)
    for i in range(4):
        end = end + counts[i]
        tile_sample = tile_sample + (tile_index >= end).astype(jnp.int32)
    for i in range(4):
        row = (tile_sample == order[i]).astype(F32)
        for half in range(2):
            mask[pl.ds(half * 128 + i * 32, 32), :] = jnp.broadcast_to(row, (32, ROWS))
    gate = jnp.tanh(jnp.full((1, HD), gate_ref[0], F32))
    query_gain = gains[0:1, :] * HD ** (-0.5)
    key_gain = gains[1:2, :]

    pl.semaphore_wait(barrier, len(greeted))

    used = [0]

    def send(src, dst, target):
        i = used[0]
        used[0] += 1
        copy = pltpu.make_async_remote_copy(
            src_ref=src, dst_ref=dst, send_sem=send_sem.at[i], recv_sem=recv_sem.at[i],
            device_id=target, device_id_type=MESH,
        )
        copy.start()
        return copy

    def here(ref, target):
        return send(ref, ref, target)

    def sent(copies):
        for copy in copies:
            copy.wait_send()

    def gather_xz(full, part, use):
        col, width = part
        cols = pl.ds(col, width)
        low, high = pl.ds(col, width // 2), pl.ds(col + width // 2, width // 2)
        a = here(full.at[c, z, xh, :, cols], xpair)
        yield
        a.wait_recv()
        up = here(full.at[c, z, :, :, cols], zup)
        down = here(full.at[c, z, :, :, cols], zdown)
        yield
        up.wait_recv()
        up2 = here(full.at[c, turn(z, 3), :, :, low], zup)
        down.wait_recv()
        down2 = here(full.at[c, turn(z, 1), :, :, high], zdown)
        yield
        up2.wait_recv()
        down2.wait_recv()
        s = here(full.at[c, :, :, :, cols], sib)
        yield
        s.wait_recv()
        use(part)
        sent([a, up, down, up2, down2, s])
        yield

    def gather_zx(full, part, use):
        col, width = part
        cols = pl.ds(col, width)
        low, high = pl.ds(col, width // 2), pl.ds(col + width // 2, width // 2)
        mine = full.at[c, z, xh, :, cols]
        up, down = here(mine, zup), here(mine, zdown)
        yield
        a = here(mine, xpair)
        yield
        up.wait_recv()
        up2 = here(full.at[c, turn(z, 3), xh, :, low], zup)
        a1 = here(full.at[c, turn(z, 3), xh, :, cols], xpair)
        down.wait_recv()
        down2 = here(full.at[c, turn(z, 1), xh, :, high], zdown)
        a2 = here(full.at[c, turn(z, 1), xh, :, cols], xpair)
        yield
        up2.wait_recv()
        down2.wait_recv()
        a3 = here(full.at[c, turn(z, 2), xh, :, cols], xpair)
        yield
        for copy in (a, a1, a2, a3):
            copy.wait_recv()
        s = here(full.at[c, :, :, :, cols], sib)
        yield
        s.wait_recv()
        use(part)
        sent([up, down, a, up2, a1, down2, a2, a3, s])
        yield

    loaded = set()

    def need(i):
        if i not in loaded:
            loaded.add(i)
            loads[i].wait()

    def use_hidden(part):
        need(0)
        at = pl.ds(*part)
        rows = hfull[:, :, :, :, at].reshape(ROWS, part[1])
        queries[...] += jnp.dot(rows, wq[at, :], preferred_element_type=F32)

    def use_cot(part):
        need(2)
        at = pl.ds(*part)
        rows = cfull[:, :, :, :, at].reshape(ROWS, part[1])
        gradout[...] += contract_last(rows, wo[:, at])

    def tblock(full, yy, xx):
        return full.at[c, yy, lax.div(xx, 2), lax.rem(xx, 2)]

    def gather_tiles():
        wide = tiles_ref[...].astype(F32)
        for j in range(8):
            for b in range(8):
                at = (j * 8 + b) * 128
                flat[pl.ds(j * 16 + b, 2, stride=8), :] = wide[:, at : at + 128]
        for j in range(8):
            til[j] = flat[j * 16 : (j + 1) * 16, :].astype(BF)
        copies = []
        for step in range(1, 8):
            j = mate(step)
            copies.append(send(til.at[j], tin.at[step], (sec, zh * 8 + j)))
        yield
        for copy in copies:
            copy.wait_recv()
        tin[0] = til[member]
        for s in range(8):
            owner = lax.rem(member + 8 - s, 8)
            flat[pl.ds(pl.multiple_of(owner * 16, 16), 16), :] = tin[s].astype(F32)
        for r in range(2):
            for b in range(8):
                block[b, pl.ds(r, 8, stride=2), :] = flat[pl.ds(r * 8 + b, 8, stride=16), :]
        own = tfull.at[c, y, xh, xl, zh, zl]
        for b in range(8):
            own[:, pl.ds(b * 128, 128)] = block[b].astype(BF)
        zs = [here(own, zup), here(own, zdown), here(own, zfar)]
        yield
        for copy in zs:
            copy.wait_recv()
        mine = tblock(tfull, y, x)
        xs = [here(mine, xup), here(mine, xdown), here(mine, xpair)]
        ups, downs = [here(mine, yup)], [here(mine, ydown)]
        for copy, by in zip(xs, (3, 1, 2)):
            yield
            copy.wait_recv()
            got = tblock(tfull, y, turn(x, by))
            ups.append(here(got, yup))
            downs.append(here(got, ydown))
        sibs = [here(tfull.at[c, y], sib)]
        far = []
        for k, by in enumerate((0, 3, 1, 2)):
            yield
            ups[k].wait_recv()
            downs[k].wait_recv()
            if k % 2 == 0:
                far.append(here(tblock(tfull, turn(y, 3), turn(x, by)), yup))
            else:
                far.append(here(tblock(tfull, turn(y, 1), turn(x, by)), ydown))
        sibs.append(here(tfull.at[c, turn(y, 3)], sib))
        sibs.append(here(tfull.at[c, turn(y, 1)], sib))
        yield
        for copy in far:
            copy.wait_recv()
        sibs.append(here(tfull.at[c, turn(y, 2)], sib))
        need(1)
        proj[...] = project(c)
        yield
        for copy in sibs:
            copy.wait_recv()
        sent(copies + zs + xs + ups + downs + far + sibs)
        yield from attend()
        yield

    def scatter_xz(full, sibin, rel, zin, xin, part, make, finish):
        col, width = part
        cols = pl.ds(col, width)
        low, high = pl.ds(col, width // 2), pl.ds(col + width // 2, width // 2)
        make(part)
        s = send(full.at[oc, :, :, :, cols], sibin.at[:, :, :, cols], sib)
        yield
        s.wait_recv()
        add_to(full.at[c, turn(z, 2), :, :, cols], sibin.at[turn(z, 2), :, :, cols])
        r0 = send(full.at[c, turn(z, 2), :, :, low], rel.at[0, :, :, low], zup)
        r1 = send(full.at[c, turn(z, 2), :, :, high], rel.at[1, :, :, high], zdown)
        for by in (1, 3, 0):
            add_to(full.at[c, turn(z, by), :, :, cols], sibin.at[turn(z, by), :, :, cols])
        yield
        r0.wait_recv()
        add_to(full.at[c, turn(z, 1), :, :, low], rel.at[0, :, :, low])
        z0 = send(full.at[c, turn(z, 1), :, :, cols], zin.at[0, :, :, cols], zup)
        r1.wait_recv()
        add_to(full.at[c, turn(z, 3), :, :, high], rel.at[1, :, :, high])
        z1 = send(full.at[c, turn(z, 3), :, :, cols], zin.at[1, :, :, cols], zdown)
        yield
        z0.wait_recv()
        z1.wait_recv()
        add_to(full.at[c, z, ox, :, cols], zin.at[0, ox, :, cols], zin.at[1, ox, :, cols])
        a = send(full.at[c, z, ox, :, cols], xin.at[0, :, cols], xpair)
        yield
        a.wait_recv()
        finish(cols, (full.at[c, z, xh, :, cols], zin.at[0, xh, :, cols], zin.at[1, xh, :, cols], xin.at[0, :, cols]))
        sent([s, r0, r1, z0, z1, a])
        yield

    def scatter_zx(full, sibin, rel, zin, xin, part, make, finish):
        col, width = part
        cols = pl.ds(col, width)
        low, high = pl.ds(col, width // 2), pl.ds(col + width // 2, width // 2)
        make(part)
        s = send(full.at[oc, :, :, :, cols], sibin.at[:, :, :, cols], sib)
        yield
        s.wait_recv()
        add_to(full.at[c, :, ox, :, cols], sibin.at[:, ox, :, cols])
        a = send(full.at[c, :, ox, :, cols], xin.at[:, :, cols], xpair)
        yield
        a.wait_recv()
        add_to(full.at[c, turn(z, 2), xh, :, cols], sibin.at[turn(z, 2), xh, :, cols], xin.at[turn(z, 2), :, cols])
        r0 = send(full.at[c, turn(z, 2), xh, :, low], rel.at[0, 0, :, low], zup)
        r1 = send(full.at[c, turn(z, 2), xh, :, high], rel.at[1, 0, :, high], zdown)
        for by in (1, 3):
            add_to(full.at[c, turn(z, by), xh, :, cols], sibin.at[turn(z, by), xh, :, cols], xin.at[turn(z, by), :, cols])
        yield
        r0.wait_recv()
        add_to(full.at[c, turn(z, 1), xh, :, low], rel.at[0, 0, :, low])
        z0 = send(full.at[c, turn(z, 1), xh, :, cols], zin.at[0, 0, :, cols], zup)
        r1.wait_recv()
        add_to(full.at[c, turn(z, 3), xh, :, high], rel.at[1, 0, :, high])
        z1 = send(full.at[c, turn(z, 3), xh, :, cols], zin.at[1, 0, :, cols], zdown)
        yield
        z0.wait_recv()
        z1.wait_recv()
        finish(cols, (full.at[c, z, xh, :, cols], sibin.at[z, xh, :, cols], xin.at[z, :, cols], zin.at[0, 0, :, cols], zin.at[1, 0, :, cols]))
        sent([s, a, r0, r1, z0, z1])
        yield

    def total(terms):
        value = terms[0][...].astype(F32)
        for term in terms[1:]:
            value = value + term[...].astype(F32)
        return value

    def make_out(part):
        at = pl.ds(*part)
        value = jnp.dot(attended[...], wo[:, at], preferred_element_type=F32)
        hfull[:, :, :, :, at] = value.astype(BF).reshape(2, 4, 2, 16, part[1])

    def finish_out(cols, terms):
        out_ref[:, cols] = (hid[:, cols].astype(F32) + gate[0:1, 0:1] * total(terms)).astype(BF)

    def make_grad(part):
        at = pl.ds(*part)
        value = contract_last(gradq[...], wq[at, :])
        cfull[:, :, :, :, at] = value.astype(BF).reshape(2, 4, 2, 16, part[1])

    def finish_grad(cols, terms):
        grad_ref[:, cols] = (cot[:, cols].astype(F32) + total(terms)).astype(BF)

    tile_sibs = []

    def make_tiles():
        for core in (oc, c):
            for h in range(2):
                for l in range(2):
                    at = pl.multiple_of((l * 4 + h * 2 + core) * 1024, 1024)
                    value = contract_last(gxout[...], wt[pl.ds(at, 1024), :])
                    tfull[core, :, h, :, :, l] = value.astype(BF).reshape(4, 2, 2, 16, 1024)
            if core is oc:
                for col in range(0, 1024, PIECE):
                    cols = pl.ds(col, PIECE)
                    tile_sibs.append(
                        send(tfull.at[oc, :, :, :, :, :, :, cols], sib_t.at[:, :, :, :, :, :, cols], sib)
                    )
            yield

    def scatter_tiles(col):
        cols = pl.ds(col, PIECE)

        def unit(ref, *index):
            return ref.at[(*index, Ellipsis, cols)]

        s = tile_sibs[col // PIECE]
        s.wait_recv()

        def merge(by):
            yy = turn(y, by)
            for h in range(2):
                add_to(tfull.at[c, yy, h, :, :, :, :, cols], sib_t.at[yy, h, :, :, :, :, cols])

        merge(2)
        r0 = send(tfull.at[c, turn(y, 2), 0, :, :, :, :, cols], yrel.at[0, :, :, :, :, cols], yup)
        r1 = send(tfull.at[c, turn(y, 2), 1, :, :, :, :, cols], yrel.at[1, :, :, :, :, cols], ydown)
        for by in (1, 3, 0):
            merge(by)
        yield
        r0.wait_recv()
        add_to(tfull.at[c, turn(y, 1), 0, :, :, :, :, cols], yrel.at[0, :, :, :, :, cols])
        y0 = send(tfull.at[c, turn(y, 1), :, :, :, :, :, cols], yin.at[0, :, :, :, :, :, cols], yup)
        r1.wait_recv()
        add_to(tfull.at[c, turn(y, 3), 1, :, :, :, :, cols], yrel.at[1, :, :, :, :, cols])
        y1 = send(tfull.at[c, turn(y, 3), :, :, :, :, :, cols], yin.at[1, :, :, :, :, :, cols], ydown)
        yield
        y0.wait_recv()
        y1.wait_recv()
        xs = []
        for k, (by, target) in enumerate(((2, xpair), (1, xup), (3, xdown), (0, None))):
            h, l = lax.div(turn(x, by), 2), lax.rem(turn(x, by), 2)
            add_to(
                tfull.at[c, y, h, l, :, :, :, cols],
                yin.at[0, h, l, :, :, :, cols],
                yin.at[1, h, l, :, :, :, cols],
            )
            if target is not None:
                xs.append(send(tfull.at[c, y, h, l, :, :, :, cols], xin_t.at[k, :, :, :, cols], target))
        yield
        for copy in xs:
            copy.wait_recv()
        zs = []
        for k, (by, target) in enumerate(((2, zfar), (1, zup), (3, zdown), (0, None))):
            h, l = lax.div(turn(z, by), 2), lax.rem(turn(z, by), 2)
            mine = tfull.at[c, y, xh, xl, h, l, :, cols]
            terms = [xin_t.at[i, h, l, :, cols] for i in range(3)]
            if target is None:
                final = total([mine] + terms)
            else:
                add_to(mine, *terms)
                zs.append(send(mine, zin_t.at[k, :, cols], target))
        yield
        for copy in zs:
            copy.wait_recv()
        final = final + total([zin_t.at[i, :, cols] for i in range(3)])
        for b in range(PIECE // 128):
            block[col // 128 + b] = final[:, b * 128 : (b + 1) * 128]
        sent([s, r0, r1, y0, y1] + xs + zs)
        yield

    def hand_out():
        for r in range(2):
            for b in range(8):
                flat[pl.ds(r * 8 + b, 8, stride=16), :] = block[b, pl.ds(r, 8, stride=2), :]
        copies = []
        for step in range(1, 8):
            j = mate(step)
            copies.append(
                send(flat.at[pl.ds(pl.multiple_of(j * 16, 16), 16), :], gin.at[step], (sec, zh * 8 + j))
            )
        yield
        gin[0] = flat[pl.ds(pl.multiple_of(member * 16, 16), 16), :]
        for copy in copies:
            copy.wait_recv()
        sent(copies)
        for s in range(8):
            owner = lax.rem(member + 8 - s, 8)
            flat[pl.ds(pl.multiple_of(owner * 16, 16), 16), :] = gin[s]
        for j in range(8):
            for b in range(8):
                tgrad_ref[:, pl.ds((j * 8 + b) * 128, 128)] = flat[pl.ds(j * 16 + b, 2, stride=8), :]
        yield

    def project(core):
        value = jnp.zeros((ROWS, HD), F32)
        for h in range(2):
            for l in range(2):
                rows = tfull[core, :, h, :, :, l].reshape(ROWS, 1024)
                at = pl.multiple_of((l * 4 + h * 2 + core) * 1024, 1024)
                value = value + jnp.dot(rows, wt[pl.ds(at, 1024), :], preferred_element_type=F32)
        return value

    def attend():
        value = proj[...] + project(oc)
        proj[...] = value
        normed = value * norm_scale(value) * key_gain
        kv[c] = jnp.where(c == 0, normed, value).astype(BF)
        kv_copy = here(kv.at[c], sib)
        yield
        for h in range(HEADS):
            sl = pl.ds(h * HD, HD)
            q = queries[:, sl]
            normedq[:, sl] = (q * norm_scale(q) * query_gain).astype(BF)
        kv_copy.wait_recv()

        keys, values = kv[0], kv[1]
        for h in range(HEADS):
            sl = pl.ds(h * HD, HD)
            scores = contract_last(normedq[:, sl], keys)
            raised = jnp.where(mask[...] > 0.0, jnp.exp(scores), 0.0)
            w = (raised / jnp.sum(raised, axis=-1, keepdims=True)).astype(BF)
            weights[h] = w
            attended[:, sl] = jnp.dot(w, values, preferred_element_type=F32).astype(BF)
        kv_copy.wait_send()

    def attend_back():
        keys, values = kv[0], kv[1]
        grad_keys = jnp.zeros((ROWS, HD), F32)
        grad_values = jnp.zeros((ROWS, HD), F32)
        for h in range(HEADS):
            sl = pl.ds(h * HD, HD)
            g = (gate * gradout[:, sl]).astype(BF)
            w = weights[h]
            wide = w.astype(F32)
            prob = contract_last(g, values)
            score = (wide * (prob - jnp.sum(wide * prob, axis=-1, keepdims=True))).astype(BF)
            q = queries[:, sl]
            back = jnp.dot(score, keys, preferred_element_type=F32)
            gradq[:, sl] = head_norm_back(q, norm_scale(q), query_gain, back).astype(BF)
            grad_keys = grad_keys + contract_first(score, normedq[:, sl])
            grad_values = grad_values + contract_first(w, g)
        gxout[...] = jnp.where(c == 0, grad_values, grad_keys).astype(BF)
        gx_copy = send(gxout, gxin, sib)
        kept = jnp.where(c == 0, grad_keys, grad_values).astype(BF).astype(F32)
        yield
        gx_copy.wait()
        both = kept + gxin[...].astype(F32)
        raw = proj[...]
        gxout[...] = jnp.where(c == 0, head_norm_back(raw, norm_scale(raw), key_gain, both), both).astype(BF)
        yield

    queries[...] = jnp.zeros_like(queries)
    gradout[...] = jnp.zeros_like(gradout)

    tasks = {"t": gather_tiles(), "bw": attend_back(), "d": make_tiles(), "l": hand_out()}
    for i in range(2):
        tasks["ha%d" % i] = gather_xz(hfull, XZ[i], use_hidden)
        tasks["hb%d" % i] = gather_zx(hfull, ZX[i], use_hidden)
        tasks["ca%d" % i] = gather_xz(cfull, XZ[i], use_cot)
        tasks["cb%d" % i] = gather_zx(cfull, ZX[i], use_cot)
        tasks["oa%d" % i] = scatter_xz(hfull, sib_o, rel_o, zin_o, xin_o, XZ[i], make_out, finish_out)
        tasks["ob%d" % i] = scatter_zx(hfull, sib_o, rel_o, zin_o, xin_o, ZX[i], make_out, finish_out)
        tasks["ga%d" % i] = scatter_xz(cfull, sib_g, rel_g, zin_g, xin_g, XZ[i], make_grad, finish_grad)
        tasks["gb%d" % i] = scatter_zx(cfull, sib_g, rel_g, zin_g, xin_g, ZX[i], make_grad, finish_grad)
    for i in range(1024 // PIECE):
        tasks["p%d" % i] = scatter_tiles(i * PIECE)
    for name in ORDER:
        next(tasks[name])


def body(hidden, tiles, tile_counts, sample_order, query_weight, tile_weight, output_weight, head_gains, cross_gate, cotangent):
    smem = pl.BlockSpec(memory_space=pltpu.SMEM)
    vmem = pl.BlockSpec(memory_space=pltpu.VMEM)
    hbm = pl.BlockSpec(memory_space=pl.ANY)
    rows = (2, 4, 2, 16, D)

    def tp_buffers():
        return [
            pltpu.VMEM((4, 2, 16, D), BF),
            pltpu.VMEM((2, 2, 16, D), BF),
            pltpu.VMEM((2, 2, 16, D), BF),
            pltpu.VMEM((4, 16, D), BF),
        ]

    copies = 224
    out, grad, tgrad = pl.pallas_call(
        kernel,
        out_shape=(
            jax.ShapeDtypeStruct((16, D), BF),
            jax.ShapeDtypeStruct((16, D), BF),
            jax.ShapeDtypeStruct((2, D), F32),
        ),
        in_specs=[smem, smem, smem, vmem, vmem, vmem, vmem, hbm, hbm, hbm],
        out_specs=(vmem, vmem, vmem),
        scratch_shapes=[
            pltpu.VMEM((D, LOCAL), BF),
            pltpu.VMEM((D, HD), BF),
            pltpu.VMEM((LOCAL, D), BF),
            pltpu.VMEM(rows, BF),
            pltpu.VMEM(rows, BF),
            pltpu.VMEM((2, 4, 2, 2, 2, 2, 16, 1024), BF),
            *tp_buffers(),
            *tp_buffers(),
            pltpu.VMEM((4, 2, 2, 2, 2, 16, 1024), BF),
            pltpu.VMEM((2, 2, 2, 2, 16, 1024), BF),
            pltpu.VMEM((2, 2, 2, 2, 2, 16, 1024), BF),
            pltpu.VMEM((3, 2, 2, 16, 1024), BF),
            pltpu.VMEM((3, 16, 1024), BF),
            pltpu.VMEM((8, 16, 128), BF),
            pltpu.VMEM((8, 16, 128), BF),
            pltpu.VMEM((128, 128), F32),
            pltpu.VMEM((8, 16, 128), F32),
            pltpu.VMEM((8, 16, 128), F32),
            pltpu.VMEM((ROWS, LOCAL), F32),
            pltpu.VMEM((ROWS, LOCAL), F32),
            pltpu.VMEM((ROWS, LOCAL), BF),
            pltpu.VMEM((HEADS, ROWS, ROWS), BF),
            pltpu.VMEM((ROWS, LOCAL), BF),
            pltpu.VMEM((ROWS, LOCAL), BF),
            pltpu.VMEM((ROWS, HD), F32),
            pltpu.VMEM((2, ROWS, HD), BF),
            pltpu.VMEM((ROWS, HD), BF),
            pltpu.VMEM((ROWS, HD), BF),
            pltpu.VMEM((ROWS, ROWS), F32),
            pltpu.SemaphoreType.DMA((3,)),
            pltpu.SemaphoreType.DMA((copies,)),
            pltpu.SemaphoreType.DMA((copies,)),
        ],
        compiler_params=pltpu.CompilerParams(
            collective_id=0, has_side_effects=True, vmem_limit_bytes=60 * 2**20
        ),
        name="cross_attention",
    )(
        tile_counts, sample_order, cross_gate, head_gains[0], hidden[0], cotangent[0], tiles,
        query_weight[0], tile_weight[0], output_weight[0],
    )
    return (out[None], grad[None], tgrad)


def solution(mesh):
    placed = (
        P("section", "tp", None),
        P(("section", "tp"), None),
        P(),
        P(),
        P("section", None, "tp"),
        P("section", None, "tp"),
        P("section", "tp", None),
        P("section", None, None),
        P("section"),
        P("section", "tp", None),
    )
    return jax.shard_map(
        body,
        mesh=mesh,
        in_specs=placed,
        out_specs=(P("section", "tp", None), P("section", "tp", None), P(("section", "tp"), None)),
        check_vma=False,
    )
```

```python
import functools
import jax
import jax.numpy as jnp
from jax import lax
from jax.experimental import pallas as pl
from jax.experimental.pallas import tpu as pltpu
from jax.sharding import PartitionSpec as P

MESH = pl.DeviceIdType.MESH
NORM_EPS = 1e-06
D = 8192
HD = 128
LOCAL = 512
HEADS = 4
ROWS = 256
BF = jnp.bfloat16
F32 = jnp.float32

XZ = ((0, 2560), (2560, 2560))
ZX = ((5120, 1536), (6656, 1536))
PIECE = 256

ORDER = (
    "t", "ca1", "ca0", "cb0", "hb0", "t", "ha1", "cb0", "cb1", "ca1", "hb0", "t", "hb0", "ca0",
    "ha1", "hb0", "t", "ca1", "ha0", "t", "cb0", "ca0", "t", "cb1", "hb1", "t", "hb0", "cb1", "t",
    "ca1", "ha0", "ca0", "hb0", "t", "hb1", "cb0", "t", "cb1", "hb1", "ha1", "ca0", "ha0", "hb1",
    "ca1", "cb0", "cb1", "ha1", "t", "ha0", "cb0", "cb1", "hb1", "ha1", "t", "ha0", "hb1", "t",
    "ob1", "bw", "oa0", "ga0", "gb0", "ob1", "bw", "d", "oa0", "ga1", "ga0", "d", "p0", "gb1", "p1",
    "gb0", "oa0", "ob0", "p3", "ob1", "oa1", "p2", "ob0", "ga1", "gb1", "p0", "oa1", "p3", "p1",
    "gb0", "ob1", "ga1", "p0", "p2", "oa1", "oa0", "ob0", "p3", "p0", "gb1", "ga0", "p1", "p2",
    "ob1", "ob0", "ga1", "oa1", "p3", "p1", "oa0", "p2", "gb1", "gb0", "ga0", "ga1", "p0", "p3",
    "p1", "p2", "l", "ob0", "oa1", "gb0", "gb1", "ga0", "l",
)


def contract_last(left, right):
    return lax.dot_general(left, right, (((1,), (1,)), ((), ())), preferred_element_type=F32)


def contract_first(left, right):
    return lax.dot_general(left, right, (((0,), (0,)), ((), ())), preferred_element_type=F32)


def norm_scale(values):
    return lax.rsqrt(jnp.mean(values * values, axis=-1, keepdims=True) + NORM_EPS)


def head_norm_back(values, scale, gain, grad):
    normed = values * scale
    scaled = grad * gain
    return scale * (scaled - normed * jnp.mean(normed * scaled, axis=-1, keepdims=True))


def add_to(total, *terms):
    value = total[...].astype(F32)
    for term in terms:
        value = value + term[...].astype(F32)
    total[...] = value.astype(total.dtype)


def kernel(
    counts, order, gate_ref, gains, hid, cot, tiles_ref, wq_hbm, wt_hbm, wo_hbm,
    out_ref, grad_ref, tgrad_ref,
    wq, wt, wo, hfull, cfull, tfull,
    sib_o, rel_o, zin_o, xin_o,
    sib_g, rel_g, zin_g, xin_g,
    sib_t, yrel, yin, xin_t, zin_t,
    til, tin, flat, block, gin,
    queries, gradout, normedq, weights, attended, gradq, proj, kv, gxin, gxout, mask,
    load_sem, send_sem, recv_sem,
):
    sec = lax.axis_index("section")
    tp = lax.axis_index("tp")
    y, xl = lax.div(sec, 2), lax.rem(sec, 2)
    z, xh, c = lax.div(tp, 4), lax.rem(lax.div(tp, 2), 2), lax.rem(tp, 2)
    x = xh * 2 + xl
    zh, zl = lax.div(z, 2), lax.rem(z, 2)
    member = lax.rem(tp, 8)
    oc, ox = 1 - c, 1 - xh

    def turn(value, by):
        return lax.rem(value + by, 4)

    def device(dx=0, dy=0, dz=0, core=None):
        nx, ny, nz = turn(x, dx), turn(y, dy), turn(z, dz)
        core = c if core is None else core
        return (ny * 2 + lax.rem(nx, 2), nz * 4 + lax.div(nx, 2) * 2 + core)

    def mate(step):
        return lax.rem(member + step, 8)

    sib = device(core=oc)
    xpair = device(dx=2)
    zup, zdown, zfar = device(dz=1), device(dz=3), device(dz=2)
    yup, ydown = device(dy=1), device(dy=3)
    xup, xdown = device(dx=1), device(dx=3)

    loads = []
    for i, (src, dst) in enumerate(((wq_hbm, wq), (wt_hbm, wt), (wo_hbm, wo))):
        loads.append(pltpu.make_async_copy(src, dst, load_sem.at[i]))
        loads[-1].start()

    barrier = pltpu.get_barrier_semaphore()
    zodd = device(dz=lax.rem(zl * 2 + 3, 4))
    greeted = [(sec, zh * 8 + mate(step)) for step in range(1, 8)]
    greeted += [zodd, zfar, yup, ydown, xup, xdown]
    for other in greeted:
        pl.semaphore_signal(barrier, inc=1, device_id=other, device_id_type=MESH)

    hfull[c, z, xh] = hid[...]
    cfull[c, z, xh] = cot[...]

    tile_index = lax.div(lax.broadcasted_iota(jnp.int32, (1, ROWS), 1), 32)
    tile_sample = jnp.zeros((1, ROWS), jnp.int32)
    end = jnp.int32(0)
    for i in range(4):
        end = end + counts[i]
        tile_sample = tile_sample + (tile_index >= end).astype(jnp.int32)
    for i in range(4):
        row = (tile_sample == order[i]).astype(F32)
        for half in range(2):
            mask[pl.ds(half * 128 + i * 32, 32), :] = jnp.broadcast_to(row, (32, ROWS))
    gate = jnp.tanh(jnp.full((1, HD), gate_ref[0], F32))
    query_gain = gains[0:1, :] * HD ** (-0.5)
    key_gain = gains[1:2, :]

    queries[...] = jnp.zeros_like(queries)
    gradout[...] = jnp.zeros_like(gradout)
    wide = tiles_ref[...].astype(F32)
    for j in range(8):
        for b in range(8):
            at = (j * 8 + b) * 128
            flat[pl.ds(j * 16 + b, 2, stride=8), :] = wide[:, at : at + 128]
    for j in range(8):
        til[j] = flat[j * 16 : (j + 1) * 16, :].astype(BF)

    pl.semaphore_wait(barrier, len(greeted))

    used = [0]

    def send(src, dst, target):
        i = used[0]
        used[0] += 1
        copy = pltpu.make_async_remote_copy(
            src_ref=src, dst_ref=dst, send_sem=send_sem.at[i], recv_sem=recv_sem.at[i],
            device_id=target, device_id_type=MESH,
        )
        copy.start()
        return copy

    def here(ref, target):
        return send(ref, ref, target)

    def sent(copies):
        for copy in copies:
            copy.wait_send()

    def gather_xz(full, part, use):
        col, width = part
        cols = pl.ds(col, width)
        low, high = pl.ds(col, width // 2), pl.ds(col + width // 2, width // 2)
        a = here(full.at[c, z, xh, :, cols], xpair)
        yield
        a.wait_recv()
        up = here(full.at[c, z, :, :, cols], zup)
        down = here(full.at[c, z, :, :, cols], zdown)
        yield
        up.wait_recv()
        up2 = here(full.at[c, turn(z, 3), :, :, low], zup)
        down.wait_recv()
        down2 = here(full.at[c, turn(z, 1), :, :, high], zdown)
        yield
        up2.wait_recv()
        down2.wait_recv()
        s = here(full.at[c, :, :, :, cols], sib)
        yield
        s.wait_recv()
        use(part)
        sent([a, up, down, up2, down2, s])
        yield

    def gather_zx(full, part, use):
        col, width = part
        cols = pl.ds(col, width)
        low, high = pl.ds(col, width // 2), pl.ds(col + width // 2, width // 2)
        mine = full.at[c, z, xh, :, cols]
        up, down = here(mine, zup), here(mine, zdown)
        yield
        a = here(mine, xpair)
        yield
        up.wait_recv()
        up2 = here(full.at[c, turn(z, 3), xh, :, low], zup)
        a1 = here(full.at[c, turn(z, 3), xh, :, cols], xpair)
        down.wait_recv()
        down2 = here(full.at[c, turn(z, 1), xh, :, high], zdown)
        a2 = here(full.at[c, turn(z, 1), xh, :, cols], xpair)
        yield
        up2.wait_recv()
        down2.wait_recv()
        a3 = here(full.at[c, turn(z, 2), xh, :, cols], xpair)
        yield
        for copy in (a, a1, a2, a3):
            copy.wait_recv()
        s = here(full.at[c, :, :, :, cols], sib)
        yield
        s.wait_recv()
        use(part)
        sent([up, down, a, up2, a1, down2, a2, a3, s])
        yield

    loaded = set()

    def need(i):
        if i not in loaded:
            loaded.add(i)
            loads[i].wait()

    def use_hidden(part):
        need(0)
        at = pl.ds(*part)
        rows = hfull[:, :, :, :, at].reshape(ROWS, part[1])
        queries[...] += jnp.dot(rows, wq[at, :], preferred_element_type=F32)

    def use_cot(part):
        need(2)
        at = pl.ds(*part)
        rows = cfull[:, :, :, :, at].reshape(ROWS, part[1])
        gradout[...] += contract_last(rows, wo[:, at])

    def tblock(full, yy, xx):
        return full.at[c, yy, lax.div(xx, 2), lax.rem(xx, 2)]

    def gather_tiles():
        copies = []
        for step in range(1, 8):
            j = mate(step)
            copies.append(send(til.at[j], tin.at[step], (sec, zh * 8 + j)))
        yield
        for copy in copies:
            copy.wait_recv()
        tin[0] = til[member]
        for s in range(8):
            owner = lax.rem(member + 8 - s, 8)
            flat[pl.ds(pl.multiple_of(owner * 16, 16), 16), :] = tin[s].astype(F32)
        for r in range(2):
            for b in range(8):
                block[b, pl.ds(r, 8, stride=2), :] = flat[pl.ds(r * 8 + b, 8, stride=16), :]
        own = tfull.at[c, y, xh, xl, zh, zl]
        for b in range(8):
            own[:, pl.ds(b * 128, 128)] = block[b].astype(BF)
        zs = [here(own, zup), here(own, zdown), here(own, zfar)]
        yield
        for copy in zs:
            copy.wait_recv()
        mine = tblock(tfull, y, x)
        xs = [here(mine, xup), here(mine, xdown), here(mine, xpair)]
        ups, downs = [here(mine, yup)], [here(mine, ydown)]
        for copy, by in zip(xs, (3, 1, 2)):
            yield
            copy.wait_recv()
            got = tblock(tfull, y, turn(x, by))
            ups.append(here(got, yup))
            downs.append(here(got, ydown))
        sibs = [here(tfull.at[c, y], sib)]
        far = []
        for k, by in enumerate((0, 3, 1, 2)):
            yield
            ups[k].wait_recv()
            downs[k].wait_recv()
            if k % 2 == 0:
                far.append(here(tblock(tfull, turn(y, 3), turn(x, by)), yup))
            else:
                far.append(here(tblock(tfull, turn(y, 1), turn(x, by)), ydown))
        sibs.append(here(tfull.at[c, turn(y, 3)], sib))
        sibs.append(here(tfull.at[c, turn(y, 1)], sib))
        yield
        for copy, by in zip(far, (0, 3, 1, 2)):
            copy.wait_recv()
            sibs.append(here(tblock(tfull, turn(y, 2), turn(x, by)), sib))
        need(1)
        proj[...] = project(c)
        yield
        for copy in sibs:
            copy.wait_recv()
        sent(copies + zs + xs + ups + downs + far + sibs)
        yield from attend()
        yield

    def scatter_xz(full, sibin, rel, zin, xin, part, make, finish):
        col, width = part
        cols = pl.ds(col, width)
        low, high = pl.ds(col, width // 2), pl.ds(col + width // 2, width // 2)
        make(part)
        s = send(full.at[oc, :, :, :, cols], sibin.at[:, :, :, cols], sib)
        yield
        s.wait_recv()
        add_to(full.at[c, turn(z, 2), :, :, cols], sibin.at[turn(z, 2), :, :, cols])
        r0 = send(full.at[c, turn(z, 2), :, :, low], rel.at[0, :, :, low], zup)
        r1 = send(full.at[c, turn(z, 2), :, :, high], rel.at[1, :, :, high], zdown)
        for by in (1, 3, 0):
            add_to(full.at[c, turn(z, by), :, :, cols], sibin.at[turn(z, by), :, :, cols])
        yield
        r0.wait_recv()
        add_to(full.at[c, turn(z, 1), :, :, low], rel.at[0, :, :, low])
        z0 = send(full.at[c, turn(z, 1), :, :, cols], zin.at[0, :, :, cols], zup)
        r1.wait_recv()
        add_to(full.at[c, turn(z, 3), :, :, high], rel.at[1, :, :, high])
        z1 = send(full.at[c, turn(z, 3), :, :, cols], zin.at[1, :, :, cols], zdown)
        yield
        z0.wait_recv()
        z1.wait_recv()
        add_to(full.at[c, z, ox, :, cols], zin.at[0, ox, :, cols], zin.at[1, ox, :, cols])
        a = send(full.at[c, z, ox, :, cols], xin.at[0, :, cols], xpair)
        yield
        a.wait_recv()
        finish(cols, (full.at[c, z, xh, :, cols], zin.at[0, xh, :, cols], zin.at[1, xh, :, cols], xin.at[0, :, cols]))
        sent([s, r0, r1, z0, z1, a])
        yield

    def scatter_zx(full, sibin, rel, zin, xin, part, make, finish):
        col, width = part
        cols = pl.ds(col, width)
        low, high = pl.ds(col, width // 2), pl.ds(col + width // 2, width // 2)
        make(part)
        s = send(full.at[oc, :, :, :, cols], sibin.at[:, :, :, cols], sib)
        yield
        s.wait_recv()
        add_to(full.at[c, :, ox, :, cols], sibin.at[:, ox, :, cols])
        a = send(full.at[c, :, ox, :, cols], xin.at[:, :, cols], xpair)
        yield
        a.wait_recv()
        add_to(full.at[c, turn(z, 2), xh, :, cols], sibin.at[turn(z, 2), xh, :, cols], xin.at[turn(z, 2), :, cols])
        r0 = send(full.at[c, turn(z, 2), xh, :, low], rel.at[0, 0, :, low], zup)
        r1 = send(full.at[c, turn(z, 2), xh, :, high], rel.at[1, 0, :, high], zdown)
        for by in (1, 3):
            add_to(full.at[c, turn(z, by), xh, :, cols], sibin.at[turn(z, by), xh, :, cols], xin.at[turn(z, by), :, cols])
        yield
        r0.wait_recv()
        add_to(full.at[c, turn(z, 1), xh, :, low], rel.at[0, 0, :, low])
        z0 = send(full.at[c, turn(z, 1), xh, :, cols], zin.at[0, 0, :, cols], zup)
        r1.wait_recv()
        add_to(full.at[c, turn(z, 3), xh, :, high], rel.at[1, 0, :, high])
        z1 = send(full.at[c, turn(z, 3), xh, :, cols], zin.at[1, 0, :, cols], zdown)
        yield
        z0.wait_recv()
        z1.wait_recv()
        finish(cols, (full.at[c, z, xh, :, cols], sibin.at[z, xh, :, cols], xin.at[z, :, cols], zin.at[0, 0, :, cols], zin.at[1, 0, :, cols]))
        sent([s, a, r0, r1, z0, z1])
        yield

    def total(terms):
        value = terms[0][...].astype(F32)
        for term in terms[1:]:
            value = value + term[...].astype(F32)
        return value

    def make_out(part):
        at = pl.ds(*part)
        value = jnp.dot(attended[...], wo[:, at], preferred_element_type=F32)
        hfull[:, :, :, :, at] = value.astype(BF).reshape(2, 4, 2, 16, part[1])

    def finish_out(cols, terms):
        out_ref[:, cols] = (hid[:, cols].astype(F32) + gate[0:1, 0:1] * total(terms)).astype(BF)

    def make_grad(part):
        at = pl.ds(*part)
        value = contract_last(gradq[...], wq[at, :])
        cfull[:, :, :, :, at] = value.astype(BF).reshape(2, 4, 2, 16, part[1])

    def finish_grad(cols, terms):
        grad_ref[:, cols] = (cot[:, cols].astype(F32) + total(terms)).astype(BF)

    tile_sibs = []

    def make_tiles():
        for core in (oc, c):
            for h in range(2):
                for l in range(2):
                    at = pl.multiple_of((l * 4 + h * 2 + core) * 1024, 1024)
                    value = contract_last(gxout[...], wt[pl.ds(at, 1024), :])
                    tfull[core, :, h, :, :, l] = value.astype(BF).reshape(4, 2, 2, 16, 1024)
            if core is oc:
                for col in range(0, 1024, PIECE):
                    cols = pl.ds(col, PIECE)
                    tile_sibs.append(
                        send(tfull.at[oc, :, :, :, :, :, :, cols], sib_t.at[:, :, :, :, :, :, cols], sib)
                    )
            yield

    def scatter_tiles(col):
        cols = pl.ds(col, PIECE)

        def unit(ref, *index):
            return ref.at[(*index, Ellipsis, cols)]

        s = tile_sibs[col // PIECE]
        s.wait_recv()

        def merge(by):
            yy = turn(y, by)
            for h in range(2):
                add_to(tfull.at[c, yy, h, :, :, :, :, cols], sib_t.at[yy, h, :, :, :, :, cols])

        merge(2)
        r0 = send(tfull.at[c, turn(y, 2), 0, :, :, :, :, cols], yrel.at[0, :, :, :, :, cols], yup)
        r1 = send(tfull.at[c, turn(y, 2), 1, :, :, :, :, cols], yrel.at[1, :, :, :, :, cols], ydown)
        for by in (1, 3, 0):
            merge(by)
        yield
        r0.wait_recv()
        add_to(tfull.at[c, turn(y, 1), 0, :, :, :, :, cols], yrel.at[0, :, :, :, :, cols])
        y0 = send(tfull.at[c, turn(y, 1), :, :, :, :, :, cols], yin.at[0, :, :, :, :, :, cols], yup)
        r1.wait_recv()
        add_to(tfull.at[c, turn(y, 3), 1, :, :, :, :, cols], yrel.at[1, :, :, :, :, cols])
        y1 = send(tfull.at[c, turn(y, 3), :, :, :, :, :, cols], yin.at[1, :, :, :, :, :, cols], ydown)
        yield
        y0.wait_recv()
        y1.wait_recv()
        xs = []
        for k, (by, target) in enumerate(((2, xpair), (1, xup), (3, xdown), (0, None))):
            h, l = lax.div(turn(x, by), 2), lax.rem(turn(x, by), 2)
            add_to(
                tfull.at[c, y, h, l, :, :, :, cols],
                yin.at[0, h, l, :, :, :, cols],
                yin.at[1, h, l, :, :, :, cols],
            )
            if target is not None:
                xs.append(send(tfull.at[c, y, h, l, :, :, :, cols], xin_t.at[k, :, :, :, cols], target))
        yield
        for copy in xs:
            copy.wait_recv()
        zs = []
        for k, (by, target) in enumerate(((2, zfar), (1, zup), (3, zdown), (0, None))):
            h, l = lax.div(turn(z, by), 2), lax.rem(turn(z, by), 2)
            mine = tfull.at[c, y, xh, xl, h, l, :, cols]
            terms = [xin_t.at[i, h, l, :, cols] for i in range(3)]
            if target is None:
                final = total([mine] + terms)
            else:
                add_to(mine, *terms)
                zs.append(send(mine, zin_t.at[k, :, cols], target))
        yield
        for copy in zs:
            copy.wait_recv()
        final = final + total([zin_t.at[i, :, cols] for i in range(3)])
        for b in range(PIECE // 128):
            block[col // 128 + b] = final[:, b * 128 : (b + 1) * 128]
        sent([s, r0, r1, y0, y1] + xs + zs)
        yield

    def hand_out():
        for r in range(2):
            for b in range(8):
                flat[pl.ds(r * 8 + b, 8, stride=16), :] = block[b, pl.ds(r, 8, stride=2), :]
        copies = []
        for step in range(1, 8):
            j = mate(step)
            copies.append(
                send(flat.at[pl.ds(pl.multiple_of(j * 16, 16), 16), :], gin.at[step], (sec, zh * 8 + j))
            )
        yield
        gin[0] = flat[pl.ds(pl.multiple_of(member * 16, 16), 16), :]
        for copy in copies:
            copy.wait_recv()
        sent(copies)
        for s in range(8):
            owner = lax.rem(member + 8 - s, 8)
            flat[pl.ds(pl.multiple_of(owner * 16, 16), 16), :] = gin[s]
        for j in range(8):
            for b in range(8):
                tgrad_ref[:, pl.ds((j * 8 + b) * 128, 128)] = flat[pl.ds(j * 16 + b, 2, stride=8), :]
        yield

    def project(core):
        value = jnp.zeros((ROWS, HD), F32)
        for h in range(2):
            for l in range(2):
                rows = tfull[core, :, h, :, :, l].reshape(ROWS, 1024)
                at = pl.multiple_of((l * 4 + h * 2 + core) * 1024, 1024)
                value = value + jnp.dot(rows, wt[pl.ds(at, 1024), :], preferred_element_type=F32)
        return value

    def attend():
        value = proj[...] + project(oc)
        proj[...] = value
        normed = value * norm_scale(value) * key_gain
        kv[c] = jnp.where(c == 0, normed, value).astype(BF)
        kv_copy = here(kv.at[c], sib)
        yield
        for h in range(HEADS):
            sl = pl.ds(h * HD, HD)
            q = queries[:, sl]
            normedq[:, sl] = (q * norm_scale(q) * query_gain).astype(BF)
        kv_copy.wait_recv()

        keys, values = kv[0], kv[1]
        for h in range(HEADS):
            sl = pl.ds(h * HD, HD)
            scores = contract_last(normedq[:, sl], keys)
            raised = jnp.where(mask[...] > 0.0, jnp.exp(scores), 0.0)
            w = (raised / jnp.sum(raised, axis=-1, keepdims=True)).astype(BF)
            weights[h] = w
            attended[:, sl] = jnp.dot(w, values, preferred_element_type=F32).astype(BF)
        kv_copy.wait_send()

    def attend_back():
        keys, values = kv[0], kv[1]
        grad_keys = jnp.zeros((ROWS, HD), F32)
        grad_values = jnp.zeros((ROWS, HD), F32)
        for h in range(HEADS):
            sl = pl.ds(h * HD, HD)
            g = (gate * gradout[:, sl]).astype(BF)
            w = weights[h]
            wide = w.astype(F32)
            prob = contract_last(g, values)
            score = (wide * (prob - jnp.sum(wide * prob, axis=-1, keepdims=True))).astype(BF)
            q = queries[:, sl]
            back = jnp.dot(score, keys, preferred_element_type=F32)
            gradq[:, sl] = head_norm_back(q, norm_scale(q), query_gain, back).astype(BF)
            grad_keys = grad_keys + contract_first(score, normedq[:, sl])
            grad_values = grad_values + contract_first(w, g)
        gxout[...] = jnp.where(c == 0, grad_values, grad_keys).astype(BF)
        gx_copy = send(gxout, gxin, sib)
        kept = jnp.where(c == 0, grad_keys, grad_values).astype(BF).astype(F32)
        yield
        gx_copy.wait()
        both = kept + gxin[...].astype(F32)
        raw = proj[...]
        gxout[...] = jnp.where(c == 0, head_norm_back(raw, norm_scale(raw), key_gain, both), both).astype(BF)
        yield

    tasks = {"t": gather_tiles(), "bw": attend_back(), "d": make_tiles(), "l": hand_out()}
    for i in range(2):
        tasks["ha%d" % i] = gather_xz(hfull, XZ[i], use_hidden)
        tasks["hb%d" % i] = gather_zx(hfull, ZX[i], use_hidden)
        tasks["ca%d" % i] = gather_xz(cfull, XZ[i], use_cot)
        tasks["cb%d" % i] = gather_zx(cfull, ZX[i], use_cot)
        tasks["oa%d" % i] = scatter_xz(hfull, sib_o, rel_o, zin_o, xin_o, XZ[i], make_out, finish_out)
        tasks["ob%d" % i] = scatter_zx(hfull, sib_o, rel_o, zin_o, xin_o, ZX[i], make_out, finish_out)
        tasks["ga%d" % i] = scatter_xz(cfull, sib_g, rel_g, zin_g, xin_g, XZ[i], make_grad, finish_grad)
        tasks["gb%d" % i] = scatter_zx(cfull, sib_g, rel_g, zin_g, xin_g, ZX[i], make_grad, finish_grad)
    for i in range(1024 // PIECE):
        tasks["p%d" % i] = scatter_tiles(i * PIECE)
    for name in ORDER:
        next(tasks[name])


def body(hidden, tiles, tile_counts, sample_order, query_weight, tile_weight, output_weight, head_gains, cross_gate, cotangent):
    smem = pl.BlockSpec(memory_space=pltpu.SMEM)
    vmem = pl.BlockSpec(memory_space=pltpu.VMEM)
    hbm = pl.BlockSpec(memory_space=pl.ANY)
    rows = (2, 4, 2, 16, D)

    def tp_buffers():
        return [
            pltpu.VMEM((4, 2, 16, D), BF),
            pltpu.VMEM((2, 2, 16, D), BF),
            pltpu.VMEM((2, 2, 16, D), BF),
            pltpu.VMEM((4, 16, D), BF),
        ]

    copies = 224
    out, grad, tgrad = pl.pallas_call(
        kernel,
        out_shape=(
            jax.ShapeDtypeStruct((16, D), BF),
            jax.ShapeDtypeStruct((16, D), BF),
            jax.ShapeDtypeStruct((2, D), F32),
        ),
        in_specs=[smem, smem, smem, vmem, vmem, vmem, vmem, hbm, hbm, hbm],
        out_specs=(vmem, vmem, vmem),
        scratch_shapes=[
            pltpu.VMEM((D, LOCAL), BF),
            pltpu.VMEM((D, HD), BF),
            pltpu.VMEM((LOCAL, D), BF),
            pltpu.VMEM(rows, BF),
            pltpu.VMEM(rows, BF),
            pltpu.VMEM((2, 4, 2, 2, 2, 2, 16, 1024), BF),
            *tp_buffers(),
            *tp_buffers(),
            pltpu.VMEM((4, 2, 2, 2, 2, 16, 1024), BF),
            pltpu.VMEM((2, 2, 2, 2, 16, 1024), BF),
            pltpu.VMEM((2, 2, 2, 2, 2, 16, 1024), BF),
            pltpu.VMEM((3, 2, 2, 16, 1024), BF),
            pltpu.VMEM((3, 16, 1024), BF),
            pltpu.VMEM((8, 16, 128), BF),
            pltpu.VMEM((8, 16, 128), BF),
            pltpu.VMEM((128, 128), F32),
            pltpu.VMEM((8, 16, 128), F32),
            pltpu.VMEM((8, 16, 128), F32),
            pltpu.VMEM((ROWS, LOCAL), F32),
            pltpu.VMEM((ROWS, LOCAL), F32),
            pltpu.VMEM((ROWS, LOCAL), BF),
            pltpu.VMEM((HEADS, ROWS, ROWS), BF),
            pltpu.VMEM((ROWS, LOCAL), BF),
            pltpu.VMEM((ROWS, LOCAL), BF),
            pltpu.VMEM((ROWS, HD), F32),
            pltpu.VMEM((2, ROWS, HD), BF),
            pltpu.VMEM((ROWS, HD), BF),
            pltpu.VMEM((ROWS, HD), BF),
            pltpu.VMEM((ROWS, ROWS), F32),
            pltpu.SemaphoreType.DMA((3,)),
            pltpu.SemaphoreType.DMA((copies,)),
            pltpu.SemaphoreType.DMA((copies,)),
        ],
        compiler_params=pltpu.CompilerParams(
            collective_id=0, has_side_effects=True, vmem_limit_bytes=60 * 2**20
        ),
        name="cross_attention",
    )(
        tile_counts, sample_order, cross_gate, head_gains[0], hidden[0], cotangent[0], tiles,
        query_weight[0], tile_weight[0], output_weight[0],
    )
    return (out[None], grad[None], tgrad)


def solution(mesh):
    placed = (
        P("section", "tp", None),
        P(("section", "tp"), None),
        P(),
        P(),
        P("section", None, "tp"),
        P("section", None, "tp"),
        P("section", "tp", None),
        P("section", None, None),
        P("section"),
        P("section", "tp", None),
    )
    return jax.shard_map(
        body,
        mesh=mesh,
        in_specs=placed,
        out_specs=(P("section", "tp", None), P("section", "tp", None), P(("section", "tp"), None)),
        check_vma=False,
    )
```
